512 devices in a mesh: ctx: 128 (over y, z, core), tp: 4 (over x).
Axes of the slice: x: 4, y: 8, z: 8, core: 2. Of those that a mesh axis runs over, the one named last changes fastest.
Arguments:
- query_rows: bfloat16 [16384, 4096], P('ctx', 'tp'), may hold values from -1.796875 to 1.796875
- key_rows: bfloat16 [16384, 4096], P('ctx', 'tp'), may hold values from -1.796875 to 1.796875
- value_rows: bfloat16 [16384, 4096], P('ctx', 'tp'), may hold values from -6 to 6
- out_grad: bfloat16 [16384, 4096], P('ctx', 'tp'), may hold values from -6 to 6
- slopes: float32 [32], P('tp'), may hold values from 5e-05 to 0.03
- norm_gain: float32 [4096], P('tp'), may hold values from 0.25 to 1.75
- doc_lengths: int32 [16], replicated, may hold values from 1 to 16, 128 in all
Outputs:
- attended: bfloat16 [16384, 4096], P('ctx', 'tp')
- query_gradient: bfloat16 [16384, 4096], P('ctx', 'tp')
- key_gradient: bfloat16 [16384, 4096], P('ctx', 'tp')
- value_gradient: bfloat16 [16384, 4096], P('ctx', 'tp')
The draws below stay inside these ranges and needn't reach their ends.
Inputs may be any that keep to these rules, and one draw needn't show every extreme that they name: `doc_lengths`: the lengths sum to 128; the longest is exactly 16.
All inputs are finite; a program needn't handle non-finite values.
Results may differ from the reference program's by a relative error of at most 0.013.
Values may be sent and summed in bfloat16 or wider, within the bound.
A program may use at most 192 MiB of HBM per device.

```python
import math
import jax
import jax.numpy as jnp
import numpy as np
from jax import lax

H = 32
HD = 128
TOK_DEV = 128
ALIGN = 128
SPAN = 16
DOCS = 16
TOKENS = 16384


def block_levels(key, dims, cuts, least, top_value):
    def one(axis_at, shards_of):
        steps = jax.random.uniform(jax.random.fold_in(jax.random.fold_in(key, 6), axis_at), (shards_of,), jnp.float32, least / len(cuts), top_value / len(cuts))
        return jnp.repeat(jnp.exp(steps), dims[axis_at] // shards_of).reshape((-1,) + (1,) * (len(dims) - axis_at - 1))

    factor_of = one(*cuts[0])
    for cut in cuts[1:]:
        factor_of = factor_of * one(*cut)
    return factor_of


def profile(amount, total, bound, skew):
    weights = [(1 << 20) // math.isqrt(grade ** skew) + 1 for grade in range(2, amount + 1)]
    spare, holding = total - bound - (amount - 1), [1] * (amount - 1)
    while spare > 0:
        free = [i for i in range(amount - 1) if holding[i] < bound]
        mass, remaining = sum([weights[i] for i in free]), spare
        for i in free:
            more = min(bound - holding[i], max(1, remaining * weights[i] // mass), spare)
            holding[i] = holding[i] + more
            spare = spare - more
    return np.array([bound] + holding)


def ragged(key, count, total, bound, lean):
    if count == 2:
        one = jax.random.randint(key, (), max(1, total - bound), min(bound, total - 1) + 1)
        return jnp.stack([one, total - one])
    sizes = jnp.asarray(profile(count, total, bound, lean), jnp.int32)
    couples = (count - 1) // 2
    giver, sink = sizes[1:1 + 2 * couples:2], sizes[2:2 + 2 * couples:2]
    room = jnp.minimum(giver - 1, bound - sink)
    shifted = jax.random.randint(jax.random.fold_in(key, 1), (couples,), 0, 1 << 20) % (room + 1)
    sizes = sizes.at[1:1 + 2 * couples:2].set(giver - shifted).at[2:2 + 2 * couples:2].set(sink + shifted)
    return sizes[jax.random.permutation(jax.random.fold_in(key, 2), count)]


def bell_draw(key, shape, spread, limit, cuts=(), kind=jnp.bfloat16):
    array = jax.random.normal(key, shape, jnp.float32) * spread
    if len(cuts) > 0:
        array = block_levels(key, shape, cuts, -0.22, 0.18) * array
    return jnp.clip(array, min=-limit, max=limit).astype(kind)


def setup_inputs(seed: int = 0) -> dict:
    seeds = jax.random.split(jax.random.key(seed), 8)
    return {
        "query_rows": bell_draw(seeds[0], (TOKENS, H * HD), 0.3, 1.796875, ((0, 128), (1, 4))),
        "key_rows": bell_draw(seeds[1], (TOKENS, H * HD), 0.3, 1.796875, ((0, 128), (1, 4))),
        "value_rows": bell_draw(seeds[2], (TOKENS, H * HD), 1.0, 6.0, ((0, 128), (1, 4))),
        "out_grad": bell_draw(seeds[3], (TOKENS, H * HD), 1.0, 6.0, ((0, 128), (1, 4))),
        "slopes": jnp.clip(jnp.exp(math.log(0.03) - 6.3969297 * jax.random.uniform(seeds[4], (H,), jnp.float32) ** block_levels(seeds[4], (H,), ((0, 4),), -0.2, 0.2)), 4.999999873689376e-05, 0.03),
        "norm_gain": jnp.clip(1.0 + 0.15 * jax.random.normal(seeds[5], (H * HD,), jnp.float32), 0.25, 1.75),
        "doc_lengths": ragged(seeds[6], DOCS, TOKENS // ALIGN, SPAN * TOK_DEV // ALIGN, 2).astype(jnp.int32),
    }


EPSILON = 1e-06

def low(values):
    return lax.optimization_barrier(values.astype(jnp.bfloat16)).astype(jnp.float32)

def decay_tables(slopes, doc_lengths, first_pos, tok_count):
    doc_ends = jnp.cumsum(doc_lengths) * ALIGN
    doc_starts = doc_ends - doc_lengths * ALIGN
    position = first_pos + jnp.arange(tok_count, dtype=jnp.int32)
    latest = lax.optimization_barrier(jnp.max(jnp.where(doc_starts[None, :] <= position[:, None], doc_starts[None, :], 0), axis=1))
    local_pos = jnp.arange(tok_count, dtype=jnp.float32)
    distance = local_pos[:, None] - local_pos[None, :]
    same_doc = (position[None, :] >= latest[:, None]) & (distance >= 0.0)
    within = jnp.where(same_doc[None], jnp.exp(-slopes[:, None, None] * jnp.maximum(distance, 0.0)[None]), 0.0)
    fresh_row = latest < first_pos
    entry_decay = jnp.where(fresh_row[None, :], jnp.exp(-slopes[:, None] * (local_pos[None, :] + 1.0)), 0.0)
    tail_decay = jnp.where((position >= latest[-1])[None, :], jnp.exp(-slopes[:, None] * (tok_count - 1.0 - local_pos[None, :])), 0.0)
    block_decay = jnp.exp(-slopes * tok_count) * jnp.where(latest[-1] < first_pos, 1.0, 0.0)
    return (within, entry_decay, tail_decay, block_decay)

def block_pass(q_rows, k_rows, v_rows, grad_rows, slopes, norm_gain, doc_lengths, block_index, state_in, grad_out):
    tok_count = q_rows.shape[0]
    heads = slopes.shape[0]
    within, entry_decay, tail_decay, block_decay = decay_tables(slopes, doc_lengths, block_index * tok_count, tok_count)
    query_heads = q_rows.astype(jnp.float32).reshape(tok_count, heads, HD)
    key_heads = k_rows.astype(jnp.float32).reshape(tok_count, heads, HD)
    value_heads = v_rows.astype(jnp.float32).reshape(tok_count, heads, HD)
    entry_column = entry_decay.T[:, :, None]
    tail_column = tail_decay.T[:, :, None]
    scores = jnp.einsum('thd,shd->hts', query_heads, key_heads)
    weight_matrix = low(scores * within)
    intra_part = jnp.einsum('xcb,bxj->cxj', weight_matrix, value_heads)
    value_decayed = low(tail_column * value_heads)
    block_local_state = jnp.einsum('cqd,cqw->qdw', key_heads, value_decayed)
    lower_state = low(state_in)
    between_blocks_term = jnp.einsum('pwq,wqz->pwz', query_heads, lower_state) * entry_column
    raw_out = intra_part + between_blocks_term
    features = heads * HD
    inverse = lax.rsqrt(lax.optimization_barrier(jnp.sum(raw_out * raw_out, axis=(1, 2))) / features + EPSILON)
    attended = (raw_out.reshape(tok_count, features) * inverse[:, None] * norm_gain).astype(jnp.bfloat16)
    scaled = (grad_rows.astype(jnp.float32) * norm_gain).reshape(tok_count, heads, HD)
    cross_sum = lax.optimization_barrier(jnp.sum(scaled * raw_out, axis=(1, 2)))
    unscaled_gradient = low(inverse[:, None, None] * scaled - (inverse ** 3 * cross_sum / features)[:, None, None] * raw_out)
    dprob = jnp.einsum('thd,shd->hts', unscaled_gradient, value_heads)
    score_gradient = low(dprob * within)
    query_decayed = low(entry_column * query_heads)
    block_local_gradient = jnp.einsum('mbr,mbz->brz', query_decayed, unscaled_gradient)
    lower_gradient = low(grad_out)
    query_gradient = jnp.einsum('xcb,bxj->cxj', score_gradient, key_heads) + jnp.einsum('spx,pqx->spq', unscaled_gradient, lower_state) * entry_column
    key_gradient = jnp.einsum('waf,awq->fwq', score_gradient, query_heads) + jnp.einsum('gnl,njl->gnj', value_heads, lower_gradient) * tail_column
    value_gradient = jnp.einsum('waf,awq->fwq', weight_matrix, unscaled_gradient) + jnp.einsum('faz,azj->faj', key_heads, lower_gradient) * tail_column
    shaped = (tok_count, features)
    return (block_local_state, block_decay, attended, block_local_gradient, query_gradient.reshape(shaped).astype(jnp.bfloat16), key_gradient.reshape(shaped).astype(jnp.bfloat16), value_gradient.reshape(shaped).astype(jnp.bfloat16))

def reference(query_rows, key_rows, value_rows, out_grad, slopes, norm_gain, doc_lengths):
    blocks = TOKENS // TOK_DEV
    features = H * HD
    shaped = (blocks, TOK_DEV, features)
    stacked = (query_rows.reshape(shaped), key_rows.reshape(shaped), value_rows.reshape(shaped), out_grad.reshape(shaped), jnp.arange(blocks, dtype=jnp.int32))
    zero_states = jnp.zeros((blocks, H, HD, HD), jnp.float32)

    def run(states_in, grads_out):

        def one_block(items):
            return block_pass(items[0], items[1], items[2], items[3], slopes, norm_gain, doc_lengths, items[4], items[5], items[6])
        return lax.map(one_block, stacked + (states_in, grads_out))
    first_pass = run(zero_states, zero_states)
    local_states, block_decays = (first_pass[0], first_pass[1])

    def forward_step(state_now, inputs):
        return (inputs[0][:, None, None] * state_now + inputs[1], state_now)
    _, states_in = lax.scan(forward_step, jnp.zeros((H, HD, HD), jnp.float32), (block_decays, local_states))
    second_pass = run(states_in, zero_states)
    attended, local_grads = (second_pass[2], second_pass[3])

    def backward_step(grad_after, inputs):
        return (inputs[1] + inputs[0][:, None, None] * grad_after, grad_after)
    _, grads_out = lax.scan(backward_step, jnp.zeros((H, HD, HD), jnp.float32), (block_decays, local_grads), reverse=True)
    third_pass = run(states_in, grads_out)
    whole = (TOKENS, features)
    return (attended.reshape(whole), third_pass[4].reshape(whole), third_pass[5].reshape(whole), third_pass[6].reshape(whole))
```

```python
import functools

import jax
import jax.numpy as jnp
from jax import lax
from jax.experimental import pallas as pl
from jax.experimental.pallas import tpu as pltpu
from jax.sharding import PartitionSpec as P

HD = 128
EPSILON = 1e-06
MESH = pl.DeviceIdType.MESH
F32 = jnp.float32
BF16 = jnp.bfloat16
HEADS = 8
HALF = 4
ZN = 8
SHARE = HALF * HD // ZN
XN = 4


def dot(a, b, ca, cb):
    return lax.dot_general(a, b, (((ca,), (cb,)), ((), ())), preferred_element_type=F32)


def kernel(
    features,
    slopes,
    doc_lengths,
    q_hbm,
    k_hbm,
    v_hbm,
    og_hbm,
    gain,
    att_hbm,
    dq_hbm,
    dk_hbm,
    dv_hbm,
    q,
    k,
    v,
    og,
    att,
    dq,
    dk,
    dv,
    weights,
    raw,
    local,
    sib_out,
    sib_in,
    share_out,
    share_in,
    carry_out,
    carry_in,
    back_out,
    back_in,
    half_out,
    state,
    sums,
    local_sem,
    out_sem,
    sib_send,
    sib_recv,
    share_send,
    share_recv,
    carry_send,
    carry_recv,
    back_send,
    back_recv,
    sums_send,
    sums_recv,
):
    ctx = lax.axis_index("ctx")
    x = lax.axis_index("tp")
    rows_y = lax.axis_size("ctx") // (2 * ZN)
    core = lax.rem(ctx, 2)
    z = lax.rem(ctx // 2, ZN)
    y = ctx // (2 * ZN)
    is0 = core == 0
    sib = (y * (2 * ZN) + z * 2 + (1 - core), x)

    def at_z(other):
        return (y * (2 * ZN) + other * 2 + core, x)

    up = (lax.rem(y + 1, rows_y) * (2 * ZN) + z * 2 + core, x)
    down = (lax.rem(y + rows_y - 1, rows_y) * (2 * ZN) + z * 2 + core, x)
    offsets = (4, 3, 5, 2, 6, 1, 7)
    ring = [lax.rem(z + d, ZN) for d in offsets]
    cross = [lax.rem(x + d, XN) for d in (2, 1, 3)]

    barrier = pltpu.get_barrier_semaphore()
    for other in ring:
        pl.semaphore_signal(barrier, 1, device_id=at_z(other), device_id_type=MESH)
    for other in cross:
        pl.semaphore_signal(barrier, 1, device_id=(ctx, other), device_id_type=MESH)
    for other in (up, down, sib):
        pl.semaphore_signal(barrier, 1, device_id=other, device_id_type=MESH)

    loads = [
        pltpu.make_async_copy(src, dst, local_sem.at[i])
        for i, (src, dst) in enumerate(((k_hbm, k), (v_hbm, v), (q_hbm, q), (og_hbm, og)))
    ]
    for load in loads:
        load.start()

    starts = [jnp.int32(0)]
    for j in range(doc_lengths.shape[0] - 1):
        starts.append(starts[-1] + doc_lengths[j])

    def carries(block):
        hit = starts[0] == block
        for start in starts[1:]:
            hit = hit | (start == block)
        return jnp.where(hit, F32(0.0), F32(1.0))

    row_first = y * (2 * ZN)
    flags = [carries(row_first + i) for i in range(2 * ZN)]
    flag0 = carries(row_first + 2 * z)
    flag1 = carries(row_first + 2 * z + 1)
    flag = jnp.where(is0, flag0, flag1)
    share_head = HALF * core + z // (ZN // HALF)
    lam_share = jnp.exp(jnp.full((1, HD), -HD * 1.0, F32) * slopes[share_head])
    lam2 = lam_share * lam_share
    step_decay = [lam2 * (flags[2 * j] * flags[2 * j + 1]) for j in range(ZN)]

    token = lax.broadcasted_iota(jnp.int32, (HD, HD), 0).astype(F32)
    column = lax.broadcasted_iota(jnp.int32, (HD, HD), 1).astype(F32)
    distance = token - column

    def within(h):
        return jnp.where(distance >= 0.0, jnp.exp(-slopes[h] * jnp.maximum(distance, 0.0)), 0.0)

    def entry(h):
        return jnp.exp(-slopes[h] * (token + 1.0)) * flag

    def tail(h):
        return jnp.exp(-slopes[h] * (HD - 1.0 - token))

    def lam_of(h):
        return jnp.exp(jnp.full((1, HD), -HD * 1.0, F32) * slopes[h])

    def cols(h):
        return pl.ds(h * HD, HD)

    mine = HALF * core
    theirs = HALF * (1 - core)

    def remote(src, dst, send, recv, device):
        return pltpu.make_async_remote_copy(
            src_ref=src,
            dst_ref=dst,
            send_sem=send,
            recv_sem=recv,
            device_id=device,
            device_id_type=MESH,
        )

    def scan(phase, backward):
        sends = []
        for other in ring:
            copy = remote(
                share_out.at[phase, other],
                share_in.at[phase, z],
                share_send.at[phase, other],
                share_recv.at[phase, z],
                at_z(other),
            )
            copy.start()
            sends.append(copy)
        share_in[phase, z] = share_out[phase, z]

        yield

        for other in ring[::-1]:
            remote(
                share_out.at[phase, z],
                share_in.at[phase, other],
                share_send.at[phase, other],
                share_recv.at[phase, other],
                at_z(other),
            ).wait_recv()
        order = range(ZN - 1, -1, -1) if backward else range(ZN)
        total = jnp.zeros((SHARE, HD), F32)
        product = jnp.ones((1, HD), F32)
        before, products = {}, {}
        for j in order:
            before[j], products[j] = total, product
            total = total * step_decay[j] + share_in[phase, j].astype(F32)
            product = product * step_decay[j]
        carry_out[phase] = total.astype(BF16)
        carry = remote(
            carry_out.at[phase],
            carry_in.at[phase],
            carry_send.at[phase],
            carry_recv.at[phase],
            down if backward else up,
        )
        carry.start()
        carry.wait_recv()
        incoming = carry_in[phase].astype(F32)
        for j in range(ZN):
            back_out[phase, j] = (before[j] + products[j] * incoming).astype(BF16)
        for other in ring:
            copy = remote(
                back_out.at[phase, other],
                back_in.at[phase, z],
                back_send.at[phase, other],
                back_recv.at[phase, z],
                at_z(other),
            )
            copy.start()
            sends.append(copy)
        back_in[phase, z] = back_out[phase, z]

        yield

        for other in ring[::-1]:
            remote(
                back_out.at[phase, z],
                back_in.at[phase, other],
                back_send.at[phase, other],
                back_recv.at[phase, other],
                at_z(other),
            ).wait_recv()
        for copy in sends:
            copy.wait_send()
        carry.wait_send()
        yield

    def head_of(buffer, phase, i):
        per = ZN // HALF
        return jnp.concatenate([buffer[phase, per * i + j] for j in range(per)], axis=0)

    def put_head(buffer, phase, i, value):
        per = ZN // HALF
        for j in range(per):
            buffer[phase, per * i + j] = value[j * SHARE : (j + 1) * SHARE]

    loads[0].wait()
    loads[1].wait()
    for h in range(HEADS):
        value_decayed = (tail(h) * v[:, cols(h)].astype(F32)).astype(BF16)
        local[h] = dot(k[:, cols(h)], value_decayed, 0, 0)
    for i in range(HALF):
        sib_out[0, i] = local[theirs + i].astype(BF16)

    pl.semaphore_wait(barrier, len(ring) + len(cross) + 3)

    sib_copy = remote(sib_out.at[0], sib_in.at[0], sib_send.at[0], sib_recv.at[0], sib)
    sib_copy.start()
    sib_copy.wait_recv()
    for i in range(HALF):
        lam = lam_of(mine + i)
        own, other = local[mine + i], sib_in[0, i].astype(F32)
        first, second = jnp.where(is0, own, other), jnp.where(is0, other, own)
        put_head(share_out, 0, i, (first * (lam * flag1) + second).astype(BF16))
    forward = scan(0, False)
    next(forward)

    loads[2].wait()
    loads[3].wait()
    for h in range(HEADS):
        scores = dot(q[:, cols(h)], k[:, cols(h)], 1, 1)
        weight = (scores * within(h)).astype(BF16)
        weights[h] = weight
        raw[:, cols(h)] = dot(weight, v[:, cols(h)], 1, 0)

    next(forward)
    next(forward)
    for i in range(HALF):
        lam = lam_of(mine + i)
        own, other = local[mine + i], sib_in[0, i].astype(F32)
        first = jnp.where(is0, own, other)
        arrived = head_of(back_in, 0, i).astype(F32)
        later = arrived * (lam * flag0) + first
        state[0, mine + i] = jnp.where(is0, arrived, later).astype(BF16)
        half_out[0, i] = jnp.where(is0, later, arrived).astype(BF16)
    half_copy = remote(
        half_out.at[0], state.at[0, pl.ds(mine, HALF)], sib_send.at[1], sib_recv.at[1], sib
    )
    half_copy.start()
    half_copy.wait_recv()

    squares = jnp.zeros((HD, HD), F32)
    products = jnp.zeros((HD, HD), F32)
    for h in range(HEADS):
        raw_h = raw[:, cols(h)] + dot(q[:, cols(h)], state[0, h], 1, 0) * entry(h)
        raw[:, cols(h)] = raw_h
        squares = squares + raw_h * raw_h
        products = products + raw_h * (og[:, cols(h)].astype(F32) * gain[:, cols(h)])
    square_row = jnp.sum(squares.T, axis=0, keepdims=True)
    product_row = jnp.sum(products.T, axis=0, keepdims=True)
    upper = lax.broadcasted_iota(jnp.int32, (8, HD), 0) < 4
    sums[x] = jnp.where(upper, square_row, product_row)
    sum_copies = []
    for other in cross:
        copy = remote(
            sums.at[x], sums.at[x], sums_send.at[other], sums_recv.at[x], (ctx, other)
        )
        copy.start()
        sum_copies.append(copy)
    for other in cross[::-1]:
        remote(
            sums.at[x], sums.at[other], sums_send.at[other], sums_recv.at[other], (ctx, other)
        ).wait_recv()
    total = sums[0] + sums[1] + sums[2] + sums[3]
    inverse_row = lax.rsqrt(total[0:1] / features + EPSILON)
    factor_row = inverse_row * inverse_row * inverse_row * total[4:5] / features
    inverse = jnp.broadcast_to(inverse_row, (HD, HD)).T
    factor = jnp.broadcast_to(factor_row, (HD, HD)).T

    for h in range(HEADS):
        scaled = og[:, cols(h)].astype(F32) * gain[:, cols(h)]
        grad = (inverse * scaled - factor * raw[:, cols(h)]).astype(BF16)
        og[:, cols(h)] = grad
        query_decayed = (entry(h) * q[:, cols(h)].astype(F32)).astype(BF16)
        local[h] = dot(query_decayed, grad, 0, 0)
    for i in range(HALF):
        sib_out[1, i] = local[theirs + i].astype(BF16)
    sib_copy2 = remote(sib_out.at[1], sib_in.at[1], sib_send.at[2], sib_recv.at[2], sib)
    sib_copy2.start()
    sib_copy2.wait_recv()
    for i in range(HALF):
        lam = lam_of(mine + i)
        own, other = local[mine + i], sib_in[1, i].astype(F32)
        first, second = jnp.where(is0, own, other), jnp.where(is0, other, own)
        put_head(share_out, 1, i, (first + second * (lam * flag0)).astype(BF16))
    backward = scan(1, True)
    next(backward)

    stores = []

    def store(src, dst):
        copy = pltpu.make_async_copy(src, dst, out_sem.at[len(stores)])
        copy.start()
        stores.append(copy)

    for h in range(HEADS):
        att[:, cols(h)] = (raw[:, cols(h)] * inverse * gain[:, cols(h)]).astype(BF16)
    store(att, att_hbm)
    for h in range(HEADS):
        grad = og[:, cols(h)]
        dscore = (dot(grad, v[:, cols(h)], 1, 1) * within(h)).astype(BF16)
        dq[:, cols(h)] = (
            dot(dscore, k[:, cols(h)], 1, 0) + dot(grad, state[0, h], 1, 1) * entry(h)
        ).astype(BF16)
        dk[:, cols(h)] = dot(dscore, q[:, cols(h)], 0, 0)
        dv[:, cols(h)] = dot(weights[h], grad, 0, 0)
    store(dq, dq_hbm)

    next(backward)
    next(backward)
    for i in range(HALF):
        lam = lam_of(mine + i)
        own, other = local[mine + i], sib_in[1, i].astype(F32)
        second = jnp.where(is0, other, own)
        arrived = head_of(back_in, 1, i).astype(F32)
        earlier = arrived * (lam * flag1) + second
        state[1, mine + i] = jnp.where(is0, earlier, arrived).astype(BF16)
        half_out[1, i] = jnp.where(is0, arrived, earlier).astype(BF16)
    half_copy2 = remote(
        half_out.at[1], state.at[1, pl.ds(mine, HALF)], sib_send.at[3], sib_recv.at[3], sib
    )
    half_copy2.start()
    half_copy2.wait_recv()

    stores[0].wait()
    stores[1].wait()
    for h in range(HEADS):
        grad_state = state[1, h]
        att[:, cols(h)] = (
            dk[:, cols(h)] + dot(v[:, cols(h)], grad_state, 1, 1) * tail(h)
        ).astype(BF16)
    store(att, dk_hbm)
    for h in range(HEADS):
        grad_state = state[1, h]
        dq[:, cols(h)] = (
            dv[:, cols(h)] + dot(k[:, cols(h)], grad_state, 1, 0) * tail(h)
        ).astype(BF16)
    store(dq, dv_hbm)

    sib_copy.wait_send()
    half_copy.wait_send()
    sib_copy2.wait_send()
    half_copy2.wait_send()
    for copy in sum_copies:
        copy.wait_send()
    stores[2].wait()
    stores[3].wait()


def body(query_rows, key_rows, value_rows, out_grad, slopes, norm_gain, doc_lengths):
    rows, width = query_rows.shape
    features = width * lax.axis_size("tp")
    whole = jax.ShapeDtypeStruct((rows, width), BF16)
    smem = pl.BlockSpec(memory_space=pltpu.SMEM)
    anywhere = pl.BlockSpec(memory_space=pl.ANY)
    dma = pltpu.SemaphoreType.DMA
    return pl.pallas_call(
        functools.partial(kernel, features),
        out_shape=(whole,) * 4,
        in_specs=[smem, smem]
        + [anywhere] * 4
        + [pl.BlockSpec(memory_space=pltpu.VMEM)],
        out_specs=(anywhere,) * 4,
        scratch_shapes=[
            pltpu.VMEM((rows, width), BF16),
            pltpu.VMEM((rows, width), BF16),
            pltpu.VMEM((rows, width), BF16),
            pltpu.VMEM((rows, width), BF16),
            pltpu.VMEM((rows, width), BF16),
            pltpu.VMEM((rows, width), BF16),
            pltpu.VMEM((rows, width), F32),
            pltpu.VMEM((rows, width), F32),
            pltpu.VMEM((HEADS, HD, HD), BF16),
            pltpu.VMEM((rows, width), F32),
            pltpu.VMEM((HEADS, HD, HD), F32),
            pltpu.VMEM((2, HALF, HD, HD), BF16),
            pltpu.VMEM((2, HALF, HD, HD), BF16),
            pltpu.VMEM((2, ZN, SHARE, HD), BF16),
            pltpu.VMEM((2, ZN, SHARE, HD), BF16),
            pltpu.VMEM((2, SHARE, HD), BF16),
            pltpu.VMEM((2, SHARE, HD), BF16),
            pltpu.VMEM((2, ZN, SHARE, HD), BF16),
            pltpu.VMEM((2, ZN, SHARE, HD), BF16),
            pltpu.VMEM((2, HALF, HD, HD), BF16),
            pltpu.VMEM((2, HEADS, HD, HD), BF16),
            pltpu.VMEM((XN, 8, HD), F32),
            dma((4,)),
            dma((4,)),
            dma((4,)),
            dma((4,)),
            dma((2, ZN)),
            dma((2, ZN)),
            dma((2,)),
            dma((2,)),
            dma((2, ZN)),
            dma((2, ZN)),
            dma((XN,)),
            dma((XN,)),
        ],
        compiler_params=pltpu.CompilerParams(
            collective_id=0, has_side_effects=True, vmem_limit_bytes=32 * 1024 * 1024
        ),
        name="lightning",
    )(
        slopes,
        doc_lengths,
        query_rows,
        key_rows,
        value_rows,
        out_grad,
        norm_gain.reshape(1, width),
    )


def solution(mesh):
    spec = P("ctx", "tp")
    in_specs = (spec, spec, spec, spec, P("tp"), P("tp"), P())
    return jax.shard_map(
        body, mesh=mesh, in_specs=in_specs, out_specs=(spec,) * 4, check_vma=False
    )
```

```python
import functools

import jax
import jax.numpy as jnp
from jax import lax
from jax.experimental import pallas as pl
from jax.experimental.pallas import tpu as pltpu
from jax.sharding import PartitionSpec as P

HD = 128
EPSILON = 1e-06
MESH = pl.DeviceIdType.MESH
F32 = jnp.float32
BF16 = jnp.bfloat16
HEADS = 8
HALF = 4
ZN = 8
SHARE = HALF * HD // ZN
XN = 4


def dot(a, b, ca, cb):
    return lax.dot_general(a, b, (((ca,), (cb,)), ((), ())), preferred_element_type=F32)


def kernel(
    features,
    slopes_hbm,
    doc_hbm,
    q_hbm,
    k_hbm,
    v_hbm,
    og_hbm,
    gain_hbm,
    att_hbm,
    dq_hbm,
    dk_hbm,
    dv_hbm,
    slopes,
    doc_lengths,
    gain_flat,
    gain,
    q,
    k,
    v,
    og,
    att,
    dq,
    dk,
    dv,
    weights,
    raw,
    local,
    sib_out,
    sib_in,
    share_out,
    share_in,
    carry_out,
    carry_in,
    back_out,
    back_in,
    half_out,
    state,
    sums,
    local_sem,
    out_sem,
    sib_send,
    sib_recv,
    share_send,
    share_recv,
    carry_send,
    carry_recv,
    back_send,
    back_recv,
    sums_send,
    sums_recv,
):
    ctx = lax.axis_index("ctx")
    x = lax.axis_index("tp")
    rows_y = lax.axis_size("ctx") // (2 * ZN)
    core = lax.rem(ctx, 2)
    z = lax.rem(ctx // 2, ZN)
    y = ctx // (2 * ZN)
    is0 = core == 0
    sib = (y * (2 * ZN) + z * 2 + (1 - core), x)

    def at_z(other):
        return (y * (2 * ZN) + other * 2 + core, x)

    up = (lax.rem(y + 1, rows_y) * (2 * ZN) + z * 2 + core, x)
    down = (lax.rem(y + rows_y - 1, rows_y) * (2 * ZN) + z * 2 + core, x)
    offsets = (4, 3, 5, 2, 6, 1, 7)
    ring = [lax.rem(z + d, ZN) for d in offsets]
    cross = [lax.rem(x + d, XN) for d in (2, 1, 3)]

    barrier = pltpu.get_barrier_semaphore()
    for other in ring:
        pl.semaphore_signal(barrier, 1, device_id=at_z(other), device_id_type=MESH)
    for other in cross:
        pl.semaphore_signal(barrier, 1, device_id=(ctx, other), device_id_type=MESH)
    for other in (up, down, sib):
        pl.semaphore_signal(barrier, 1, device_id=other, device_id_type=MESH)

    loads = [
        pltpu.make_async_copy(src, dst, local_sem.at[i])
        for i, (src, dst) in enumerate(
            (
                (k_hbm, k),
                (v_hbm, v),
                (q_hbm, q),
                (og_hbm, og),
                (slopes_hbm, slopes),
                (doc_hbm, doc_lengths),
                (gain_hbm, gain_flat),
            )
        )
    ]
    for load in loads:
        load.start()

    for load in loads[4:]:
        load.wait()
    for h in range(HEADS):
        gain[:, h * HD : (h + 1) * HD] = gain_flat[h * HD : (h + 1) * HD].reshape(1, HD)

    starts = [jnp.int32(0)]
    for j in range(doc_lengths.shape[0] - 1):
        starts.append(starts[-1] + doc_lengths[j])

    def carries(block):
        hit = starts[0] == block
        for start in starts[1:]:
            hit = hit | (start == block)
        return jnp.where(hit, F32(0.0), F32(1.0))

    row_first = y * (2 * ZN)
    flags = [carries(row_first + i) for i in range(2 * ZN)]
    flag0 = carries(row_first + 2 * z)
    flag1 = carries(row_first + 2 * z + 1)
    flag = jnp.where(is0, flag0, flag1)
    share_head = HALF * core + z // (ZN // HALF)
    lam_share = jnp.exp(jnp.full((1, HD), -HD * 1.0, F32) * slopes[share_head])
    lam2 = lam_share * lam_share
    step_decay = [lam2 * (flags[2 * j] * flags[2 * j + 1]) for j in range(ZN)]

    token = lax.broadcasted_iota(jnp.int32, (HD, HD), 0).astype(F32)
    column = lax.broadcasted_iota(jnp.int32, (HD, HD), 1).astype(F32)
    distance = token - column

    def within(h):
        return jnp.where(distance >= 0.0, jnp.exp(-slopes[h] * jnp.maximum(distance, 0.0)), 0.0)

    def entry(h):
        return jnp.exp(-slopes[h] * (token + 1.0)) * flag

    def tail(h):
        return jnp.exp(-slopes[h] * (HD - 1.0 - token))

    def lam_of(h):
        return jnp.exp(jnp.full((1, HD), -HD * 1.0, F32) * slopes[h])

    def cols(h):
        return pl.ds(h * HD, HD)

    mine = HALF * core
    theirs = HALF * (1 - core)

    def remote(src, dst, send, recv, device):
        return pltpu.make_async_remote_copy(
            src_ref=src,
            dst_ref=dst,
            send_sem=send,
            recv_sem=recv,
            device_id=device,
            device_id_type=MESH,
        )

    def scan(phase, backward):
        sends = []
        for other in ring:
            copy = remote(
                share_out.at[phase, other],
                share_in.at[phase, z],
                share_send.at[phase, other],
                share_recv.at[phase, z],
                at_z(other),
            )
            copy.start()
            sends.append(copy)
        share_in[phase, z] = share_out[phase, z]

        yield

        for other in ring[::-1]:
            remote(
                share_out.at[phase, z],
                share_in.at[phase, other],
                share_send.at[phase, other],
                share_recv.at[phase, other],
                at_z(other),
            ).wait_recv()
        order = range(ZN - 1, -1, -1) if backward else range(ZN)
        total = jnp.zeros((SHARE, HD), F32)
        product = jnp.ones((1, HD), F32)
        before, products = {}, {}
        for j in order:
            before[j], products[j] = total, product
            total = total * step_decay[j] + share_in[phase, j].astype(F32)
            product = product * step_decay[j]
        carry_out[phase] = total.astype(BF16)
        carry = remote(
            carry_out.at[phase],
            carry_in.at[phase],
            carry_send.at[phase],
            carry_recv.at[phase],
            down if backward else up,
        )
        carry.start()
        carry.wait_recv()
        incoming = carry_in[phase].astype(F32)
        for j in range(ZN):
            back_out[phase, j] = (before[j] + products[j] * incoming).astype(BF16)
        for other in ring:
            copy = remote(
                back_out.at[phase, other],
                back_in.at[phase, z],
                back_send.at[phase, other],
                back_recv.at[phase, z],
                at_z(other),
            )
            copy.start()
            sends.append(copy)
        back_in[phase, z] = back_out[phase, z]

        yield

        for other in ring[::-1]:
            remote(
                back_out.at[phase, z],
                back_in.at[phase, other],
                back_send.at[phase, other],
                back_recv.at[phase, other],
                at_z(other),
            ).wait_recv()
        for copy in sends:
            copy.wait_send()
        carry.wait_send()
        yield

    def head_of(buffer, phase, i):
        per = ZN // HALF
        return jnp.concatenate([buffer[phase, per * i + j] for j in range(per)], axis=0)

    def put_head(buffer, phase, i, value):
        per = ZN // HALF
        for j in range(per):
            buffer[phase, per * i + j] = value[j * SHARE : (j + 1) * SHARE]

    loads[0].wait()
    loads[1].wait()
    for h in range(HEADS):
        value_decayed = (tail(h) * v[:, cols(h)].astype(F32)).astype(BF16)
        local[h] = dot(k[:, cols(h)], value_decayed, 0, 0)
    for i in range(HALF):
        sib_out[0, i] = local[theirs + i].astype(BF16)

    pl.semaphore_wait(barrier, len(ring) + len(cross) + 3)

    sib_copy = remote(sib_out.at[0], sib_in.at[0], sib_send.at[0], sib_recv.at[0], sib)
    sib_copy.start()
    sib_copy.wait_recv()
    for i in range(HALF):
        lam = lam_of(mine + i)
        own, other = local[mine + i], sib_in[0, i].astype(F32)
        first, second = jnp.where(is0, own, other), jnp.where(is0, other, own)
        put_head(share_out, 0, i, (first * (lam * flag1) + second).astype(BF16))
    forward = scan(0, False)
    next(forward)

    loads[2].wait()
    loads[3].wait()
    for h in range(HEADS):
        scores = dot(q[:, cols(h)], k[:, cols(h)], 1, 1)
        weight = (scores * within(h)).astype(BF16)
        weights[h] = weight
        raw[:, cols(h)] = dot(weight, v[:, cols(h)], 1, 0)

    next(forward)
    next(forward)
    for i in range(HALF):
        lam = lam_of(mine + i)
        own, other = local[mine + i], sib_in[0, i].astype(F32)
        first = jnp.where(is0, own, other)
        arrived = head_of(back_in, 0, i).astype(F32)
        later = arrived * (lam * flag0) + first
        state[0, mine + i] = jnp.where(is0, arrived, later).astype(BF16)
        half_out[0, i] = jnp.where(is0, later, arrived).astype(BF16)
    half_copy = remote(
        half_out.at[0], state.at[0, pl.ds(mine, HALF)], sib_send.at[1], sib_recv.at[1], sib
    )
    half_copy.start()
    half_copy.wait_recv()

    squares = jnp.zeros((HD, HD), F32)
    products = jnp.zeros((HD, HD), F32)
    for h in range(HEADS):
        raw_h = raw[:, cols(h)] + dot(q[:, cols(h)], state[0, h], 1, 0) * entry(h)
        raw[:, cols(h)] = raw_h
        squares = squares + raw_h * raw_h
        products = products + raw_h * (og[:, cols(h)].astype(F32) * gain[:, cols(h)])
    square_row = jnp.sum(squares.T, axis=0, keepdims=True)
    product_row = jnp.sum(products.T, axis=0, keepdims=True)
    upper = lax.broadcasted_iota(jnp.int32, (8, HD), 0) < 4
    sums[x] = jnp.where(upper, square_row, product_row)
    sum_copies = []
    for other in cross:
        copy = remote(
            sums.at[x], sums.at[x], sums_send.at[other], sums_recv.at[x], (ctx, other)
        )
        copy.start()
        sum_copies.append(copy)
    for other in cross[::-1]:
        remote(
            sums.at[x], sums.at[other], sums_send.at[other], sums_recv.at[other], (ctx, other)
        ).wait_recv()
    total = sums[0] + sums[1] + sums[2] + sums[3]
    inverse_row = lax.rsqrt(total[0:1] / features + EPSILON)
    factor_row = inverse_row * inverse_row * inverse_row * total[4:5] / features
    inverse = jnp.broadcast_to(inverse_row, (HD, HD)).T
    factor = jnp.broadcast_to(factor_row, (HD, HD)).T

    for h in range(HEADS):
        scaled = og[:, cols(h)].astype(F32) * gain[:, cols(h)]
        grad = (inverse * scaled - factor * raw[:, cols(h)]).astype(BF16)
        og[:, cols(h)] = grad
        query_decayed = (entry(h) * q[:, cols(h)].astype(F32)).astype(BF16)
        local[h] = dot(query_decayed, grad, 0, 0)
    for i in range(HALF):
        sib_out[1, i] = local[theirs + i].astype(BF16)
    sib_copy2 = remote(sib_out.at[1], sib_in.at[1], sib_send.at[2], sib_recv.at[2], sib)
    sib_copy2.start()
    sib_copy2.wait_recv()
    for i in range(HALF):
        lam = lam_of(mine + i)
        own, other = local[mine + i], sib_in[1, i].astype(F32)
        first, second = jnp.where(is0, own, other), jnp.where(is0, other, own)
        put_head(share_out, 1, i, (first + second * (lam * flag0)).astype(BF16))
    backward = scan(1, True)
    next(backward)

    stores = []

    def store(src, dst):
        copy = pltpu.make_async_copy(src, dst, out_sem.at[len(stores)])
        copy.start()
        stores.append(copy)

    for h in range(HEADS):
        att[:, cols(h)] = (raw[:, cols(h)] * inverse * gain[:, cols(h)]).astype(BF16)
    store(att, att_hbm)
    for h in range(HEADS):
        grad = og[:, cols(h)]
        dscore = (dot(grad, v[:, cols(h)], 1, 1) * within(h)).astype(BF16)
        dq[:, cols(h)] = (
            dot(dscore, k[:, cols(h)], 1, 0) + dot(grad, state[0, h], 1, 1) * entry(h)
        ).astype(BF16)
        dk[:, cols(h)] = dot(dscore, q[:, cols(h)], 0, 0)
        dv[:, cols(h)] = dot(weights[h], grad, 0, 0)
    store(dq, dq_hbm)

    next(backward)
    next(backward)
    for i in range(HALF):
        lam = lam_of(mine + i)
        own, other = local[mine + i], sib_in[1, i].astype(F32)
        second = jnp.where(is0, other, own)
        arrived = head_of(back_in, 1, i).astype(F32)
        earlier = arrived * (lam * flag1) + second
        state[1, mine + i] = jnp.where(is0, earlier, arrived).astype(BF16)
        half_out[1, i] = jnp.where(is0, arrived, earlier).astype(BF16)
    half_copy2 = remote(
        half_out.at[1], state.at[1, pl.ds(mine, HALF)], sib_send.at[3], sib_recv.at[3], sib
    )
    half_copy2.start()
    half_copy2.wait_recv()

    stores[0].wait()
    stores[1].wait()
    for h in range(HEADS):
        grad_state = state[1, h]
        att[:, cols(h)] = (
            dk[:, cols(h)] + dot(v[:, cols(h)], grad_state, 1, 1) * tail(h)
        ).astype(BF16)
    store(att, dk_hbm)
    for h in range(HEADS):
        grad_state = state[1, h]
        dq[:, cols(h)] = (
            dv[:, cols(h)] + dot(k[:, cols(h)], grad_state, 1, 0) * tail(h)
        ).astype(BF16)
    store(dq, dv_hbm)

    sib_copy.wait_send()
    half_copy.wait_send()
    sib_copy2.wait_send()
    half_copy2.wait_send()
    for copy in sum_copies:
        copy.wait_send()
    stores[2].wait()
    stores[3].wait()


def place(*refs):
    sources, targets, sems = refs[:4], refs[4:8], refs[8]
    copies = [
        pltpu.make_async_copy(src, dst, sems.at[i])
        for i, (src, dst) in enumerate(zip(sources, targets))
    ]
    for copy in copies:
        copy.start()
    for copy in copies:
        copy.wait()


def body(query_rows, key_rows, value_rows, out_grad, slopes, norm_gain, doc_lengths):
    rows, width = query_rows.shape
    features = width * lax.axis_size("tp")
    whole = jax.ShapeDtypeStruct((rows, width), BF16)
    anywhere = pl.BlockSpec(memory_space=pl.ANY)
    dma = pltpu.SemaphoreType.DMA
    results = pl.pallas_call(
        functools.partial(kernel, features),
        out_shape=(whole,) * 4,
        in_specs=[anywhere] * 7,
        out_specs=(anywhere,) * 4,
        scratch_shapes=[
            pltpu.SMEM(slopes.shape, F32),
            pltpu.SMEM(doc_lengths.shape, jnp.int32),
            pltpu.VMEM((width,), F32),
            pltpu.VMEM((1, width), F32),
            pltpu.VMEM((rows, width), BF16),
            pltpu.VMEM((rows, width), BF16),
            pltpu.VMEM((rows, width), BF16),
            pltpu.VMEM((rows, width), BF16),
            pltpu.VMEM((rows, width), BF16),
            pltpu.VMEM((rows, width), BF16),
            pltpu.VMEM((rows, width), F32),
            pltpu.VMEM((rows, width), F32),
            pltpu.VMEM((HEADS, HD, HD), BF16),
            pltpu.VMEM((rows, width), F32),
            pltpu.VMEM((HEADS, HD, HD), F32),
            pltpu.VMEM((2, HALF, HD, HD), BF16),
            pltpu.VMEM((2, HALF, HD, HD), BF16),
            pltpu.VMEM((2, ZN, SHARE, HD), BF16),
            pltpu.VMEM((2, ZN, SHARE, HD), BF16),
            pltpu.VMEM((2, SHARE, HD), BF16),
            pltpu.VMEM((2, SHARE, HD), BF16),
            pltpu.VMEM((2, ZN, SHARE, HD), BF16),
            pltpu.VMEM((2, ZN, SHARE, HD), BF16),
            pltpu.VMEM((2, HALF, HD, HD), BF16),
            pltpu.VMEM((2, HEADS, HD, HD), BF16),
            pltpu.VMEM((XN, 8, HD), F32),
            dma((7,)),
            dma((4,)),
            dma((4,)),
            dma((4,)),
            dma((2, ZN)),
            dma((2, ZN)),
            dma((2,)),
            dma((2,)),
            dma((2, ZN)),
            dma((2, ZN)),
            dma((XN,)),
            dma((XN,)),
        ],
        compiler_params=pltpu.CompilerParams(
            collective_id=0, has_side_effects=True, vmem_limit_bytes=60 * 1024 * 1024
        ),
        name="lightning",
    )(
        slopes,
        doc_lengths,
        query_rows,
        key_rows,
        value_rows,
        out_grad,
        norm_gain,
    )
    return pl.pallas_call(
        place,
        out_shape=(whole,) * 4,
        in_specs=[anywhere] * 4,
        out_specs=(anywhere,) * 4,
        scratch_shapes=[dma((4,))],
        compiler_params=pltpu.CompilerParams(vmem_limit_bytes=60 * 1024 * 1024),
        name="place",
    )(*results)


def solution(mesh):
    spec = P("ctx", "tp")
    in_specs = (spec, spec, spec, spec, P("tp"), P("tp"), P())
    return jax.shard_map(
        body, mesh=mesh, in_specs=in_specs, out_specs=(spec,) * 4, check_vma=False
    )
```

```python
import functools

import jax
import jax.numpy as jnp
from jax import lax
from jax.experimental import pallas as pl
from jax.experimental.pallas import tpu as pltpu
from jax.sharding import PartitionSpec as P

HD = 128
EPSILON = 1e-06
MESH = pl.DeviceIdType.MESH
F32 = jnp.float32
BF16 = jnp.bfloat16
TOK = 128
PAIR = 2 * TOK
HALF = 4
WIDE = HALF * HD
ZN = 8
SHARE = HALF * HD // ZN
PER = ZN // HALF
XN = 4


def dot(a, b, ca, cb):
    return lax.dot_general(a, b, (((ca,), (cb,)), ((), ())), preferred_element_type=F32)


def kernel(
    features,
    slopes_hbm,
    doc_hbm,
    q_hbm,
    k_hbm,
    v_hbm,
    og_hbm,
    gain_hbm,
    att_out,
    dq_out,
    dk_out,
    dv_out,
    slopes,
    doc_lengths,
    gain_flat,
    gain,
    q,
    k,
    v,
    og,
    k_other,
    v_other,
    att,
    dq,
    dk,
    dv,
    table,
    weights,
    raw,
    dk_part,
    dv_part,
    share_out,
    share_in,
    carry_out,
    carry_in,
    back_out,
    back_in,
    sums,
    local_sem,
    own_sem,
    swap_send,
    swap_recv,
    share_send,
    share_recv,
    carry_send,
    carry_recv,
    back_send,
    back_recv,
    sums_send,
    sums_recv,
    result_send,
    result_recv,
):
    ctx = lax.axis_index("ctx")
    x = lax.axis_index("tp")
    rows_y = lax.axis_size("ctx") // (2 * ZN)
    core = lax.rem(ctx, 2)
    z = lax.rem(ctx // 2, ZN)
    y = ctx // (2 * ZN)

    def device(dx, y_at, z_at, core_at):
        return (y_at * (2 * ZN) + z_at * 2 + core_at, lax.rem(x + dx, XN))

    sib = device(0, y, z, 1 - core)
    up = device(0, lax.rem(y + 1, rows_y), z, core)
    down = device(0, lax.rem(y + rows_y - 1, rows_y), z, core)
    ring = [lax.rem(z + d, ZN) for d in (4, 3, 5, 2, 6, 1, 7)]
    heads_of = [(2, 1), (2, 0), (1, 1), (3, 1), (1, 0), (3, 0), (0, 1)]
    cross = [
        (2 * lax.rem(x + dx, XN) + lax.rem(core + dc, 2), device(dx, y, z, lax.rem(core + dc, 2)))
        for dx, dc in heads_of
    ]

    def at_z(other):
        return device(0, y, other, core)

    barrier = pltpu.get_barrier_semaphore()
    partners = [at_z(other) for other in ring] + [up, down] + [target for _, target in cross]
    for partner in partners:
        pl.semaphore_signal(barrier, 1, device_id=partner, device_id_type=MESH)

    mine = pl.ds(pl.multiple_of(core * WIDE, WIDE), WIDE)
    theirs = pl.ds(pl.multiple_of((1 - core) * WIDE, WIDE), WIDE)
    own = pl.ds(pl.multiple_of(core * TOK, TOK), TOK)
    other_rows = pl.ds(pl.multiple_of((1 - core) * TOK, TOK), TOK)

    loads = [
        pltpu.make_async_copy(src, dst, local_sem.at[i])
        for i, (src, dst) in enumerate(
            (
                (k_hbm.at[:, theirs], k_other),
                (v_hbm.at[:, theirs], v_other),
                (k_hbm.at[:, mine], k.at[own]),
                (v_hbm.at[:, mine], v.at[own]),
                (slopes_hbm, slopes),
                (doc_hbm, doc_lengths),
                (gain_hbm, gain_flat),
                (q_hbm.at[:, mine], q.at[own]),
                (og_hbm.at[:, mine], og.at[own]),
            )
        )
    ]
    for load in loads:
        load.start()

    def remote(src, dst, send, recv, target):
        return pltpu.make_async_remote_copy(
            src_ref=src,
            dst_ref=dst,
            send_sem=send,
            recv_sem=recv,
            device_id=target,
            device_id_type=MESH,
        )

    swaps = [
        remote(src, dst.at[own], swap_send.at[i], swap_recv.at[i], sib)
        for i, (src, dst) in enumerate(
            ((k_other, k), (v_other, v), (q_hbm.at[:, theirs], q), (og_hbm.at[:, theirs], og))
        )
    ]

    for load in loads[4:7]:
        load.wait()

    starts = [jnp.int32(0)]
    for j in range(doc_lengths.shape[0] - 1):
        starts.append(starts[-1] + doc_lengths[j])

    def carries(block):
        hit = starts[0] == block
        for start in starts[1:]:
            hit = hit | (start == block)
        return jnp.where(hit, F32(0.0), F32(1.0))

    flag0 = carries(y * (2 * ZN) + 2 * z)
    flag1 = carries(y * (2 * ZN) + 2 * z + 1)
    slope = [slopes[HALF * core + i] for i in range(HALF)]
    for i in range(HALF):
        begin = pl.multiple_of(core * WIDE + i * HD, HD)
        gain[:, i * HD : (i + 1) * HD] = gain_flat[pl.ds(begin, HD)].reshape(1, HD)

    token = lax.broadcasted_iota(jnp.int32, (PAIR, HD), 0)
    second = token >= TOK
    token_f = token.astype(F32)
    entry_flag = jnp.where(second, flag0 * flag1, flag0)
    tail_flag = jnp.where(second, 1.0, flag1)

    def entry(i):
        return jnp.exp(-slope[i] * (token_f + 1.0)) * entry_flag

    def tail(i):
        return jnp.exp(-slope[i] * (PAIR - 1.0 - token_f)) * tail_flag

    def cols(i):
        return slice(i * HD, (i + 1) * HD)

    row = lax.broadcasted_iota(jnp.int32, (PAIR, PAIR), 0)
    column = lax.broadcasted_iota(jnp.int32, (PAIR, PAIR), 1)
    distance = (row - column).astype(F32)
    reach = jnp.where((row >= TOK) & (column < TOK), flag1, 1.0)
    for i in range(HALF):
        table[i] = jnp.where(
            distance >= 0.0, jnp.exp(-slope[i] * jnp.maximum(distance, 0.0)) * reach, 0.0
        )

    share_slope = slopes[HALF * core + z // PER]
    lam2 = jnp.exp(jnp.full((1, HD), -1.0 * PAIR, F32) * share_slope)
    step_decay = [
        lam2 * (carries(y * (2 * ZN) + 2 * j) * carries(y * (2 * ZN) + 2 * j + 1))
        for j in range(ZN)
    ]

    def scan(phase, backward):
        sends = []
        for other in ring:
            copy = remote(
                share_out.at[phase, other],
                share_in.at[phase, z],
                share_send.at[phase, other],
                share_recv.at[phase, z],
                at_z(other),
            )
            copy.start()
            sends.append(copy)
        share_in[phase, z] = share_out[phase, z]

        yield

        for other in ring[::-1]:
            remote(
                share_out.at[phase, z],
                share_in.at[phase, other],
                share_send.at[phase, other],
                share_recv.at[phase, other],
                at_z(other),
            ).wait_recv()
        order = range(ZN - 1, -1, -1) if backward else range(ZN)
        total = jnp.zeros((SHARE, HD), F32)
        product = jnp.ones((1, HD), F32)
        before, products = {}, {}
        for j in order:
            before[j], products[j] = total, product
            total = total * step_decay[j] + share_in[phase, j].astype(F32)
            product = product * step_decay[j]
        carry_out[phase] = total.astype(BF16)
        carry = remote(
            carry_out.at[phase],
            carry_in.at[phase],
            carry_send.at[phase],
            carry_recv.at[phase],
            down if backward else up,
        )
        carry.start()
        carry.wait_recv()
        incoming = carry_in[phase].astype(F32)
        for j in range(ZN):
            back_out[phase, j] = (before[j] + products[j] * incoming).astype(BF16)
        for other in ring:
            copy = remote(
                back_out.at[phase, other],
                back_in.at[phase, z],
                back_send.at[phase, other],
                back_recv.at[phase, z],
                at_z(other),
            )
            copy.start()
            sends.append(copy)
        back_in[phase, z] = back_out[phase, z]

        yield

        for other in ring[::-1]:
            remote(
                back_out.at[phase, z],
                back_in.at[phase, other],
                back_send.at[phase, other],
                back_recv.at[phase, other],
                at_z(other),
            ).wait_recv()
        for copy in sends:
            copy.wait_send()
        carry.wait_send()
        yield

    def state(phase, i):
        return jnp.concatenate([back_in[phase, PER * i + j] for j in range(PER)], axis=0)

    def put_shares(phase, i, value):
        for j in range(PER):
            share_out[phase, PER * i + j] = value[j * SHARE : (j + 1) * SHARE].astype(BF16)

    loads[0].wait()
    loads[1].wait()
    pl.semaphore_wait(barrier, len(partners))
    for swap in swaps:
        swap.start()
    loads[2].wait()
    loads[3].wait()
    swaps[0].wait_recv()
    swaps[1].wait_recv()
    for i in range(HALF):
        value_decayed = (tail(i) * v[:, cols(i)].astype(F32)).astype(BF16)
        put_shares(0, i, dot(k[:, cols(i)], value_decayed, 0, 0))
    forward = scan(0, False)
    next(forward)

    loads[7].wait()
    loads[8].wait()
    swaps[2].wait_recv()
    swaps[3].wait_recv()
    for i in range(HALF):
        weight = (dot(q[:, cols(i)], k[:, cols(i)], 1, 1) * table[i]).astype(BF16)
        weights[i] = weight
        raw[:, cols(i)] = dot(weight, v[:, cols(i)], 1, 0)

    next(forward)
    next(forward)
    squares = jnp.zeros((PAIR, HD), F32)
    products = jnp.zeros((PAIR, HD), F32)
    for i in range(HALF):
        raw_i = raw[:, cols(i)] + dot(q[:, cols(i)], state(0, i), 1, 0) * entry(i)
        raw[:, cols(i)] = raw_i
        squares = squares + raw_i * raw_i
        products = products + raw_i * (og[:, cols(i)].astype(F32) * gain[:, cols(i)])

    def token_row(values):
        return jnp.sum(values.T, axis=0, keepdims=True)

    place = lax.broadcasted_iota(jnp.int32, (8, HD), 0)
    slot = 2 * x + core
    sums[slot] = jnp.where(
        place < 4,
        jnp.where(place < 2, token_row(squares[:TOK]), token_row(squares[TOK:])),
        jnp.where(place < 6, token_row(products[:TOK]), token_row(products[TOK:])),
    )
    sum_copies = []
    for index, target in cross:
        copy = remote(
            sums.at[slot], sums.at[slot], sums_send.at[index], sums_recv.at[slot], target
        )
        copy.start()
        sum_copies.append(copy)
    for index, target in cross[::-1]:
        remote(
            sums.at[slot], sums.at[index], sums_send.at[index], sums_recv.at[index], target
        ).wait_recv()
    total = sums[0]
    for j in range(1, 2 * XN):
        total = total + sums[j]
    inverse_rows = lax.rsqrt(total[0:4] / features + EPSILON)
    factor_rows = inverse_rows * inverse_rows * inverse_rows * total[4:8] / features

    def token_columns(rows):
        return jnp.concatenate(
            [jnp.broadcast_to(rows[j : j + 1], (HD, HD)).T for j in (0, 2)], axis=0
        )

    inverse = token_columns(inverse_rows)
    factor = token_columns(factor_rows)

    for i in range(HALF):
        scaled = og[:, cols(i)].astype(F32) * gain[:, cols(i)]
        grad = (inverse * scaled - factor * raw[:, cols(i)]).astype(BF16)
        og[:, cols(i)] = grad
        query_decayed = (entry(i) * q[:, cols(i)].astype(F32)).astype(BF16)
        put_shares(1, i, dot(query_decayed, grad, 0, 0))
    backward = scan(1, True)
    next(backward)

    results = []

    def deliver(source, target):
        j = len(results) // 2
        keep = pltpu.make_async_copy(source.at[own], target.at[:, mine], own_sem.at[j])
        send = remote(
            source.at[other_rows], target.at[:, mine], result_send.at[j], result_recv.at[j], sib
        )
        send.start()
        keep.start()
        results.extend((keep, send))

    for i in range(HALF):
        att[:, cols(i)] = (raw[:, cols(i)] * inverse * gain[:, cols(i)]).astype(BF16)
    deliver(att, att_out)
    for i in range(HALF):
        grad = og[:, cols(i)]
        dscore = (dot(grad, v[:, cols(i)], 1, 1) * table[i]).astype(BF16)
        dq[:, cols(i)] = (
            dot(dscore, k[:, cols(i)], 1, 0) + dot(grad, state(0, i), 1, 1) * entry(i)
        ).astype(BF16)
        dk_part[:, cols(i)] = dot(dscore, q[:, cols(i)], 0, 0)
        dv_part[:, cols(i)] = dot(weights[i], grad, 0, 0)
    deliver(dq, dq_out)

    next(backward)
    next(backward)
    for i in range(HALF):
        dk[:, cols(i)] = (
            dk_part[:, cols(i)] + dot(v[:, cols(i)], state(1, i), 1, 1) * tail(i)
        ).astype(BF16)
    deliver(dk, dk_out)
    for i in range(HALF):
        dv[:, cols(i)] = (
            dv_part[:, cols(i)] + dot(k[:, cols(i)], state(1, i), 1, 0) * tail(i)
        ).astype(BF16)
    deliver(dv, dv_out)

    for swap in swaps:
        swap.wait_send()
    for copy in sum_copies:
        copy.wait_send()
    for copy in results:
        copy.wait()


def place_results(*refs):
    sources, targets, sems = refs[:4], refs[4:8], refs[8]
    copies = [
        pltpu.make_async_copy(src, dst, sems.at[i])
        for i, (src, dst) in enumerate(zip(sources, targets))
    ]
    for copy in copies:
        copy.start()
    for copy in copies:
        copy.wait()


def body(query_rows, key_rows, value_rows, out_grad, slopes, norm_gain, doc_lengths):
    rows, width = query_rows.shape
    features = width * lax.axis_size("tp")
    whole = jax.ShapeDtypeStruct((rows, width), BF16)
    in_hbm = pl.BlockSpec(memory_space=pltpu.HBM)
    in_vmem = pl.BlockSpec(memory_space=pltpu.VMEM)
    dma = pltpu.SemaphoreType.DMA
    pair_bf16 = pltpu.VMEM((PAIR, WIDE), BF16)
    pair_f32 = pltpu.VMEM((PAIR, WIDE), F32)
    shares = pltpu.VMEM((2, ZN, SHARE, HD), BF16)
    carry = pltpu.VMEM((2, SHARE, HD), BF16)
    results = pl.pallas_call(
        functools.partial(kernel, features),
        out_shape=(pltpu.VMEM((rows, width), BF16),) * 4,
        in_specs=[in_hbm] * 7,
        out_specs=(in_vmem,) * 4,
        scratch_shapes=[
            pltpu.SMEM(slopes.shape, F32),
            pltpu.SMEM(doc_lengths.shape, jnp.int32),
            pltpu.VMEM((width,), F32),
            pltpu.VMEM((1, WIDE), F32),
            pair_bf16,
            pair_bf16,
            pair_bf16,
            pair_bf16,
            pltpu.VMEM((TOK, WIDE), BF16),
            pltpu.VMEM((TOK, WIDE), BF16),
            pair_bf16,
            pair_bf16,
            pair_bf16,
            pair_bf16,
            pltpu.VMEM((HALF, PAIR, PAIR), F32),
            pltpu.VMEM((HALF, PAIR, PAIR), BF16),
            pair_f32,
            pair_f32,
            pair_f32,
            shares,
            shares,
            carry,
            carry,
            shares,
            shares,
            pltpu.VMEM((2 * XN, 8, HD), F32),
            dma((9,)),
            dma((4,)),
            dma((4,)),
            dma((4,)),
            dma((2, ZN)),
            dma((2, ZN)),
            dma((2,)),
            dma((2,)),
            dma((2, ZN)),
            dma((2, ZN)),
            dma((2 * XN,)),
            dma((2 * XN,)),
            dma((4,)),
            dma((4,)),
        ],
        compiler_params=pltpu.CompilerParams(
            collective_id=0, has_side_effects=True, vmem_limit_bytes=48 * 1024 * 1024
        ),
        name="lightning",
    )(
        *(
            pltpu.with_memory_space_constraint(a, pltpu.HBM)
            for a in (slopes, doc_lengths, query_rows, key_rows, value_rows, out_grad, norm_gain)
        )
    )
    return pl.pallas_call(
        place_results,
        out_shape=(whole,) * 4,
        in_specs=[in_vmem] * 4,
        out_specs=(in_hbm,) * 4,
        scratch_shapes=[dma((4,))],
        name="place",
    )(*results)


def solution(mesh):
    spec = P("ctx", "tp")
    in_specs = (spec, spec, spec, spec, P("tp"), P("tp"), P())
    return jax.shard_map(
        body, mesh=mesh, in_specs=in_specs, out_specs=(spec,) * 4, check_vma=False
    )
```

```python
import functools

import jax
import jax.numpy as jnp
from jax import lax
from jax.experimental import pallas as pl
from jax.experimental.pallas import tpu as pltpu
from jax.sharding import PartitionSpec as P

HD = 128
EPSILON = 1e-06
MESH = pl.DeviceIdType.MESH
F32 = jnp.float32
BF16 = jnp.bfloat16
TOK = 128
PAIR = 2 * TOK
HALF = 4
WIDE = HALF * HD
ZN = 8
SHARE = HALF * HD // ZN
PER = ZN // HALF
XN = 4


def dot(a, b, ca, cb):
    return lax.dot_general(a, b, (((ca,), (cb,)), ((), ())), preferred_element_type=F32)


def kernel(
    features,
    slopes_hbm,
    doc_hbm,
    q_hbm,
    k_hbm,
    v_hbm,
    og_hbm,
    gain_hbm,
    att_out,
    dq_out,
    dk_out,
    dv_out,
    slopes,
    doc_lengths,
    gain_flat,
    gain,
    q,
    k,
    v,
    og,
    k_other,
    v_other,
    att,
    dq,
    last,
    entries,
    tails,
    local,
    local_other,
    local_in,
    table,
    weights,
    raw,
    dk_part,
    dv_part,
    share_out,
    share_in,
    carry_out,
    carry_in,
    back_out,
    back_in,
    sums,
    local_sem,
    own_sem,
    swap_send,
    swap_recv,
    share_send,
    share_recv,
    carry_send,
    carry_recv,
    back_send,
    back_recv,
    sums_send,
    sums_recv,
    result_send,
    result_recv,
    last_send,
    last_recv,
):
    ctx = lax.axis_index("ctx")
    x = lax.axis_index("tp")
    rows_y = lax.axis_size("ctx") // (2 * ZN)
    core = lax.rem(ctx, 2)
    z = lax.rem(ctx // 2, ZN)
    y = ctx // (2 * ZN)

    def device(dx, y_at, z_at, core_at):
        return (y_at * (2 * ZN) + z_at * 2 + core_at, lax.rem(x + dx, XN))

    sib = device(0, y, z, 1 - core)
    up = device(0, lax.rem(y + 1, rows_y), z, core)
    down = device(0, lax.rem(y + rows_y - 1, rows_y), z, core)
    ring = [lax.rem(z + d, ZN) for d in (4, 3, 5, 2, 6, 1, 7)]
    heads_of = [(2, 1), (2, 0), (1, 1), (3, 1), (1, 0), (3, 0), (0, 1)]
    cross = [
        (2 * lax.rem(x + dx, XN) + lax.rem(core + dc, 2), device(dx, y, z, lax.rem(core + dc, 2)))
        for dx, dc in heads_of
    ]

    def at_z(other):
        return device(0, y, other, core)

    barrier = pltpu.get_barrier_semaphore()
    partners = [at_z(other) for other in ring] + [up, down] + [target for _, target in cross]
    for partner in partners:
        pl.semaphore_signal(barrier, 1, device_id=partner, device_id_type=MESH)

    mine = pl.ds(pl.multiple_of(core * WIDE, WIDE), WIDE)
    theirs = pl.ds(pl.multiple_of((1 - core) * WIDE, WIDE), WIDE)
    own = pl.ds(pl.multiple_of(core * TOK, TOK), TOK)
    other_rows = pl.ds(pl.multiple_of((1 - core) * TOK, TOK), TOK)

    loads = [
        pltpu.make_async_copy(src, dst, local_sem.at[i])
        for i, (src, dst) in enumerate(
            (
                (k_hbm.at[:, theirs], k_other),
                (v_hbm.at[:, theirs], v_other),
                (k_hbm.at[:, mine], k.at[own]),
                (v_hbm.at[:, mine], v.at[own]),
                (slopes_hbm, slopes),
                (doc_hbm, doc_lengths),
                (gain_hbm, gain_flat),
                (q_hbm.at[:, mine], q.at[own]),
                (og_hbm.at[:, mine], og.at[own]),
            )
        )
    ]
    for load in loads:
        load.start()

    def remote(src, dst, send, recv, target):
        return pltpu.make_async_remote_copy(
            src_ref=src,
            dst_ref=dst,
            send_sem=send,
            recv_sem=recv,
            device_id=target,
            device_id_type=MESH,
        )

    swaps = [
        remote(src, dst.at[own], swap_send.at[i], swap_recv.at[i], sib)
        for i, (src, dst) in enumerate(
            ((k_other, k), (v_other, v), (q_hbm.at[:, theirs], q), (og_hbm.at[:, theirs], og))
        )
    ]
    state_swap = remote(local_other, local_in, swap_send.at[4], swap_recv.at[4], sib)

    for load in loads[4:7]:
        load.wait()

    starts = [jnp.int32(0)]
    for j in range(doc_lengths.shape[0] - 1):
        starts.append(starts[-1] + doc_lengths[j])

    def carries(block):
        hit = starts[0] == block
        for start in starts[1:]:
            hit = hit | (start == block)
        return jnp.where(hit, F32(0.0), F32(1.0))

    flag0 = carries(y * (2 * ZN) + 2 * z)
    flag1 = carries(y * (2 * ZN) + 2 * z + 1)
    slope = [slopes[HALF * core + i] for i in range(HALF)]
    for i in range(HALF):
        begin = pl.multiple_of(core * WIDE + i * HD, HD)
        gain[:, i * HD : (i + 1) * HD] = gain_flat[pl.ds(begin, HD)].reshape(1, HD)

    def cols(i):
        return pl.ds(pl.multiple_of(i * HD, HD), HD)

    is0 = core == 0
    to_end = (TOK - 1.0) - lax.broadcasted_iota(jnp.int32, (TOK, HD), 0).astype(F32)
    to_end = to_end + jnp.where(is0, F32(TOK), F32(0.0))
    end_flag = jnp.where(is0, flag1, F32(1.0))

    def local_state(keys, values, head):
        kept = jnp.exp(-slopes[head] * to_end) * end_flag
        return dot(keys, (kept * values.astype(F32)).astype(BF16), 0, 0)

    loads[0].wait()
    loads[1].wait()
    for i in range(HALF):
        local_other[i] = local_state(
            k_other[:, cols(i)], v_other[:, cols(i)], HALF * (1 - core) + i
        ).astype(BF16)
    loads[2].wait()
    loads[3].wait()
    for i in range(HALF):
        local[i] = local_state(k[own, cols(i)], v[own, cols(i)], HALF * core + i)

    far = lax.rem(z // PER + HALF // 2, HALF)
    near = z // PER
    between = [lax.rem(far + d, HALF) for d in (1, 3)]
    next_door = z + 1 - 2 * lax.rem(z, 2)
    send_order = [far] + between + [near]
    use_order = [near] + between[::-1] + [far]

    def shares_of(i):
        return [next_door] if i is near else [PER * i + j for j in range(PER)]

    share_slope = slopes[HALF * core + z // PER]
    lam2 = jnp.exp(jnp.full((1, HD), -1.0 * PAIR, F32) * share_slope)
    step_decay = [
        lam2 * (carries(y * (2 * ZN) + 2 * j) * carries(y * (2 * ZN) + 2 * j + 1))
        for j in range(ZN)
    ]

    def share_copy(phase, other):
        return remote(
            share_out.at[phase, other],
            share_in.at[phase, z],
            share_send.at[phase, other],
            share_recv.at[phase, z],
            at_z(other),
        )

    def back_copy(phase, other):
        return remote(
            back_out.at[phase, other],
            back_in.at[phase, z],
            back_send.at[phase, other],
            back_recv.at[phase, z],
            at_z(other),
        )

    def send_shares(phase, i, value):
        share_out[phase, pl.ds(PER * i, PER)] = value.astype(BF16).reshape(PER, SHARE, HD)
        for other in shares_of(i):
            share_copy(phase, other).start()
        if i is near:
            share_in[phase, z] = share_out[phase, z]

    def turn(phase, backward):
        for other in ring[::-1]:
            remote(
                share_out.at[phase, z],
                share_in.at[phase, other],
                share_send.at[phase, other],
                share_recv.at[phase, other],
                at_z(other),
            ).wait_recv()
        order = range(ZN - 1, -1, -1) if backward else range(ZN)
        total = jnp.zeros((SHARE, HD), F32)
        product = jnp.ones((1, HD), F32)
        before, products = {}, {}
        for j in order:
            before[j], products[j] = total, product
            total = total * step_decay[j] + share_in[phase, j].astype(F32)
            product = product * step_decay[j]
        carry_out[phase] = total.astype(BF16)
        carry = remote(
            carry_out.at[phase],
            carry_in.at[phase],
            carry_send.at[phase],
            carry_recv.at[phase],
            down if backward else up,
        )
        carry.start()
        carry.wait_recv()
        incoming = carry_in[phase].astype(F32)
        for j in range(ZN):
            back_out[phase, j] = (before[j] + products[j] * incoming).astype(BF16)
        for other in ring:
            back_copy(phase, other).start()
        back_in[phase, z] = back_out[phase, z]
        for other in ring:
            share_copy(phase, other).wait_send()
        carry.wait_send()

    def arrived(phase, i):
        for other in shares_of(i):
            remote(
                back_out.at[phase, z],
                back_in.at[phase, other],
                back_send.at[phase, other],
                back_recv.at[phase, other],
                at_z(other),
            ).wait_recv()
        return state(phase, i)

    def state(phase, i):
        return back_in[phase, pl.ds(PER * i, PER)].reshape(HD, HD)

    pl.semaphore_wait(barrier, len(partners))
    state_swap.start()
    state_swap.wait_recv()
    for i in send_order:
        send_shares(0, i, local[i] + local_in[i].astype(F32))
    for swap in swaps:
        swap.start()

    token = lax.broadcasted_iota(jnp.int32, (PAIR, HD), 0)
    second = token >= TOK
    token_f = token.astype(F32)
    entry_flag = jnp.where(second, flag0 * flag1, flag0)
    tail_flag = jnp.where(second, 1.0, flag1)
    row = lax.broadcasted_iota(jnp.int32, (PAIR, PAIR), 0)
    column = lax.broadcasted_iota(jnp.int32, (PAIR, PAIR), 1)
    distance = (row - column).astype(F32)
    reach = jnp.where((row >= TOK) & (column < TOK), flag1, 1.0)
    for i in range(HALF):
        entries[i] = jnp.exp(-slope[i] * (token_f + 1.0)) * entry_flag
        tails[i] = jnp.exp(-slope[i] * (PAIR - 1.0 - token_f)) * tail_flag
        table[i] = jnp.where(
            distance >= 0.0, jnp.exp(-slope[i] * jnp.maximum(distance, 0.0)) * reach, 0.0
        )
    for load in loads[7:]:
        load.wait()
    for swap in swaps:
        swap.wait_recv()
    for i in range(HALF):
        weight = (dot(q[:, cols(i)], k[:, cols(i)], 1, 1) * table[i]).astype(BF16)
        weights[i] = weight
        raw[:, cols(i)] = dot(weight, v[:, cols(i)], 1, 0)

    turn(0, False)
    squares = jnp.zeros((PAIR, HD), F32)
    products = jnp.zeros((PAIR, HD), F32)
    for i in use_order:
        raw_i = raw[:, cols(i)] + dot(q[:, cols(i)], arrived(0, i), 1, 0) * entries[i]
        raw[:, cols(i)] = raw_i
        squares = squares + raw_i * raw_i
        products = products + raw_i * (og[:, cols(i)].astype(F32) * gain[:, cols(i)])

    def token_row(values):
        return jnp.sum(values.T, axis=0, keepdims=True)

    place = lax.broadcasted_iota(jnp.int32, (8, HD), 0)
    slot = 2 * x + core
    sums[slot] = jnp.where(
        place < 4,
        jnp.where(place < 2, token_row(squares[:TOK]), token_row(squares[TOK:])),
        jnp.where(place < 6, token_row(products[:TOK]), token_row(products[TOK:])),
    )
    sum_copies = []
    for index, target in cross:
        copy = remote(
            sums.at[slot], sums.at[slot], sums_send.at[index], sums_recv.at[slot], target
        )
        copy.start()
        sum_copies.append(copy)
    for index, target in cross[::-1]:
        remote(
            sums.at[slot], sums.at[index], sums_send.at[index], sums_recv.at[index], target
        ).wait_recv()
    total = sums[0]
    for j in range(1, 2 * XN):
        total = total + sums[j]
    inverse_rows = lax.rsqrt(total[0:4] / features + EPSILON)
    factor_rows = inverse_rows * inverse_rows * inverse_rows * total[4:8] / features

    def token_columns(rows):
        return jnp.concatenate(
            [jnp.broadcast_to(rows[j : j + 1], (HD, HD)).T for j in (0, 2)], axis=0
        )

    inverse = token_columns(inverse_rows)
    factor = token_columns(factor_rows)

    for i in send_order:
        scaled = og[:, cols(i)].astype(F32) * gain[:, cols(i)]
        grad = (inverse * scaled - factor * raw[:, cols(i)]).astype(BF16)
        og[:, cols(i)] = grad
        query_decayed = (entries[i] * q[:, cols(i)].astype(F32)).astype(BF16)
        send_shares(1, i, dot(query_decayed, grad, 0, 0))

    results = []

    def deliver(source, target):
        j = len(results) // 2
        keep = pltpu.make_async_copy(source.at[own], target.at[:, mine], own_sem.at[j])
        send = remote(
            source.at[other_rows], target.at[:, mine], result_send.at[j], result_recv.at[j], sib
        )
        send.start()
        keep.start()
        results.extend((keep, send))

    for i in range(HALF):
        att[:, cols(i)] = (raw[:, cols(i)] * inverse * gain[:, cols(i)]).astype(BF16)
    deliver(att, att_out)
    for i in range(HALF):
        grad = og[:, cols(i)]
        dscore = (dot(grad, v[:, cols(i)], 1, 1) * table[i]).astype(BF16)
        dq[:, cols(i)] = (
            dot(dscore, k[:, cols(i)], 1, 0) + dot(grad, state(0, i), 1, 1) * entries[i]
        ).astype(BF16)
        dk_part[:, cols(i)] = dot(dscore, q[:, cols(i)], 0, 0)
        dv_part[:, cols(i)] = dot(weights[i], grad, 0, 0)
    deliver(dq, dq_out)

    turn(1, True)

    def finish(j, i, value, target):
        value = value.astype(BF16)
        place_at = pl.ds(pl.multiple_of(core * WIDE + i * HD, HD), HD)
        target[:, place_at] = jnp.where(is0, value[:TOK], value[TOK:])
        last[j, i] = jnp.where(is0, value[TOK:], value[:TOK])
        return remote(
            last.at[j, i], target.at[:, place_at], last_send.at[j, i], last_recv.at[j, i], sib
        )

    finals = []
    for i in use_order:
        grad_state = arrived(1, i)
        for j, (part, operand, side, target) in enumerate(
            ((dk_part, v, 1, dk_out), (dv_part, k, 0, dv_out))
        ):
            copy = finish(
                j,
                i,
                part[:, cols(i)] + dot(operand[:, cols(i)], grad_state, 1, side) * tails[i],
                target,
            )
            copy.start()
            finals.append(copy)

    for swap in swaps + [state_swap]:
        swap.wait_send()
    for copy in sum_copies:
        copy.wait_send()
    for phase in range(2):
        for other in ring:
            back_copy(phase, other).wait_send()
    for copy in results + finals:
        copy.wait()


def place_results(*refs):
    sources, targets, sems = refs[:4], refs[4:8], refs[8]
    copies = [
        pltpu.make_async_copy(src, dst, sems.at[i])
        for i, (src, dst) in enumerate(zip(sources, targets))
    ]
    for copy in copies:
        copy.start()
    for copy in copies:
        copy.wait()


def body(query_rows, key_rows, value_rows, out_grad, slopes, norm_gain, doc_lengths):
    rows, width = query_rows.shape
    features = width * lax.axis_size("tp")
    whole = jax.ShapeDtypeStruct((rows, width), BF16)
    in_hbm = pl.BlockSpec(memory_space=pltpu.HBM)
    in_vmem = pl.BlockSpec(memory_space=pltpu.VMEM)
    dma = pltpu.SemaphoreType.DMA
    pair_bf16 = pltpu.VMEM((PAIR, WIDE), BF16)
    pair_f32 = pltpu.VMEM((PAIR, WIDE), F32)
    shares = pltpu.VMEM((2, ZN, SHARE, HD), BF16)
    carry = pltpu.VMEM((2, SHARE, HD), BF16)
    results = pl.pallas_call(
        functools.partial(kernel, features),
        out_shape=(pltpu.VMEM((rows, width), BF16),) * 4,
        in_specs=[in_hbm] * 7,
        out_specs=(in_vmem,) * 4,
        scratch_shapes=[
            pltpu.SMEM(slopes.shape, F32),
            pltpu.SMEM(doc_lengths.shape, jnp.int32),
            pltpu.VMEM((width,), F32),
            pltpu.VMEM((1, WIDE), F32),
            pair_bf16,
            pair_bf16,
            pair_bf16,
            pair_bf16,
            pltpu.VMEM((TOK, WIDE), BF16),
            pltpu.VMEM((TOK, WIDE), BF16),
            pair_bf16,
            pair_bf16,
            pltpu.VMEM((2, HALF, TOK, HD), BF16),
            pltpu.VMEM((HALF, PAIR, HD), F32),
            pltpu.VMEM((HALF, PAIR, HD), F32),
            pltpu.VMEM((HALF, HD, HD), F32),
            pltpu.VMEM((HALF, HD, HD), BF16),
            pltpu.VMEM((HALF, HD, HD), BF16),
            pltpu.VMEM((HALF, PAIR, PAIR), F32),
            pltpu.VMEM((HALF, PAIR, PAIR), BF16),
            pair_f32,
            pair_f32,
            pair_f32,
            shares,
            shares,
            carry,
            carry,
            shares,
            shares,
            pltpu.VMEM((2 * XN, 8, HD), F32),
            dma((9,)),
            dma((2,)),
            dma((5,)),
            dma((5,)),
            dma((2, ZN)),
            dma((2, ZN)),
            dma((2,)),
            dma((2,)),
            dma((2, ZN)),
            dma((2, ZN)),
            dma((2 * XN,)),
            dma((2 * XN,)),
            dma((2,)),
            dma((2,)),
            dma((2, HALF)),
            dma((2, HALF)),
        ],
        compiler_params=pltpu.CompilerParams(
            collective_id=0, has_side_effects=True, vmem_limit_bytes=48 * 1024 * 1024
        ),
        name="lightning",
    )(
        *(
            pltpu.with_memory_space_constraint(a, pltpu.HBM)
            for a in (slopes, doc_lengths, query_rows, key_rows, value_rows, out_grad, norm_gain)
        )
    )
    return pl.pallas_call(
        place_results,
        out_shape=(whole,) * 4,
        in_specs=[in_vmem] * 4,
        out_specs=(in_hbm,) * 4,
        scratch_shapes=[dma((4,))],
        compiler_params=pltpu.CompilerParams(vmem_limit_bytes=8 * 1024 * 1024),
        name="place",
    )(*(pltpu.with_memory_space_constraint(a, pltpu.VMEM) for a in results))


def solution(mesh):
    spec = P("ctx", "tp")
    in_specs = (spec, spec, spec, spec, P("tp"), P("tp"), P())
    return jax.shard_map(
        body, mesh=mesh, in_specs=in_specs, out_specs=(spec,) * 4, check_vma=False
    )
```

```python
import functools

import jax
import jax.numpy as jnp
from jax import lax
from jax.experimental import pallas as pl
from jax.experimental.pallas import tpu as pltpu
from jax.sharding import PartitionSpec as P

HD = 128
EPSILON = 1e-06
MESH = pl.DeviceIdType.MESH
F32 = jnp.float32
BF16 = jnp.bfloat16
TOK = 128
PAIR = 2 * TOK
HALF = 4
WIDE = HALF * HD
ZN = 8
SHARE = HALF * HD // ZN
PER = ZN // HALF
XN = 4


def dot(a, b, ca, cb):
    return lax.dot_general(a, b, (((ca,), (cb,)), ((), ())), preferred_element_type=F32)


def kernel(
    features,
    slopes_hbm,
    doc_hbm,
    q_hbm,
    k_hbm,
    v_hbm,
    og_hbm,
    gain_hbm,
    att_out,
    dq_out,
    dk_out,
    dv_out,
    slopes,
    doc_lengths,
    gain_flat,
    gain,
    q,
    k,
    v,
    og,
    k_other,
    v_other,
    att,
    dq,
    last,
    entries,
    tails,
    local,
    local_other,
    local_in,
    table,
    weights,
    raw,
    dk_part,
    dv_part,
    share_out,
    share_in,
    carry_out,
    carry_in,
    back_out,
    back_in,
    sums,
    answers,
    local_sem,
    own_sem,
    swap_send,
    swap_recv,
    share_send,
    share_recv,
    carry_send,
    carry_recv,
    back_send,
    back_recv,
    sums_send,
    sums_recv,
    result_send,
    result_recv,
    last_send,
    last_recv,
):
    ctx = lax.axis_index("ctx")
    x = lax.axis_index("tp")
    rows_y = lax.axis_size("ctx") // (2 * ZN)
    core = lax.rem(ctx, 2)
    z = lax.rem(ctx // 2, ZN)
    y = ctx // (2 * ZN)

    def device(dx, y_at, z_at, core_at):
        return (y_at * (2 * ZN) + z_at * 2 + core_at, lax.rem(x + dx, XN))

    sib = device(0, y, z, 1 - core)
    ring = [lax.rem(z + d, ZN) for d in (4, 3, 5, 2, 6, 1, 7)]
    heads_of = [(2, 1), (2, 0), (1, 1), (3, 1), (1, 0), (3, 0), (0, 1)]
    cross = [
        (2 * lax.rem(x + dx, XN) + lax.rem(core + dc, 2), device(dx, y, z, lax.rem(core + dc, 2)))
        for dx, dc in heads_of
    ]

    next_y, last_y = lax.rem(y + 1, rows_y), lax.rem(y + rows_y - 1, rows_y)

    def at_z(other):
        return device(0, y, other, core)

    def above(other):
        return device(0, next_y, other, core)

    def below(other):
        return device(0, last_y, other, core)


    mine = pl.ds(pl.multiple_of(core * WIDE, WIDE), WIDE)
    theirs = pl.ds(pl.multiple_of((1 - core) * WIDE, WIDE), WIDE)
    own = pl.ds(pl.multiple_of(core * TOK, TOK), TOK)
    other_rows = pl.ds(pl.multiple_of((1 - core) * TOK, TOK), TOK)

    loads = [
        pltpu.make_async_copy(src, dst, local_sem.at[i])
        for i, (src, dst) in enumerate(
            (
                (k_hbm.at[:, theirs], k_other),
                (v_hbm.at[:, theirs], v_other),
                (slopes_hbm, slopes),
                (doc_hbm, doc_lengths),
                (k_hbm.at[:, mine], k.at[own]),
                (v_hbm.at[:, mine], v.at[own]),
                (gain_hbm, gain_flat),
                (q_hbm.at[:, mine], q.at[own]),
                (og_hbm.at[:, mine], og.at[own]),
            )
        )
    ]
    for load in loads[:4]:
        load.start()

    barrier = pltpu.get_barrier_semaphore()
    along_z = [(other, at_z(other)) for other in ring]
    along_y = [(next_y, above(z)), (last_y, below(z))]
    along_x = [(index // 2, target) for index, target in cross[:-1]]

    def signal_if(condition, semaphore, target):
        @pl.when(condition)
        def _():
            pl.semaphore_signal(semaphore, 1, device_id=target, device_id_type=MESH)

    pl.semaphore_signal(barrier, 1, device_id=sib, device_id_type=MESH)
    for here, partners in ((z, along_z), (y, along_y), (x, along_x)):
        for other, target in partners:
            signal_if(other > here, barrier, target)
    lower_y = (next_y < y).astype(jnp.int32) + (last_y < y).astype(jnp.int32)
    greetings = 1 + z + lower_y + 2 * x

    def wait_some(semaphore, count):
        @pl.when(count > 0)
        def _():
            pl.semaphore_wait(semaphore, count)

    def answer():
        for other, target in along_z:
            signal_if(other < z, answers.at[z], target)
        for axis, here, partners in ((ZN, y, along_y), (ZN + 1, x, along_x)):
            for other, target in partners:
                signal_if(other < here, answers.at[axis], target)

    for load in loads[4:]:
        load.start()
    pl.semaphore_wait(barrier, greetings)
    answer()

    def remote(src, dst, send, recv, target):
        return pltpu.make_async_remote_copy(
            src_ref=src,
            dst_ref=dst,
            send_sem=send,
            recv_sem=recv,
            device_id=target,
            device_id_type=MESH,
        )

    swaps = [
        remote(src, dst.at[own], swap_send.at[i], swap_recv.at[i], sib)
        for i, (src, dst) in enumerate(
            ((k_other, k), (v_other, v), (q_hbm.at[:, theirs], q), (og_hbm.at[:, theirs], og))
        )
    ]
    state_swap = remote(local_other, local_in, swap_send.at[4], swap_recv.at[4], sib)

    for load in loads[2:4]:
        load.wait()

    starts = [jnp.int32(0)]
    for j in range(doc_lengths.shape[0] - 1):
        starts.append(starts[-1] + doc_lengths[j])

    def carries(block):
        hit = starts[0] == block
        for start in starts[1:]:
            hit = hit | (start == block)
        return jnp.where(hit, F32(0.0), F32(1.0))

    flag0 = carries(y * (2 * ZN) + 2 * z)
    flag1 = carries(y * (2 * ZN) + 2 * z + 1)
    slope = [slopes[HALF * core + i] for i in range(HALF)]
    def cols(i):
        return pl.ds(pl.multiple_of(i * HD, HD), HD)

    is0 = core == 0
    to_end = (TOK - 1.0) - lax.broadcasted_iota(jnp.int32, (TOK, HD), 0).astype(F32)
    to_end = to_end + jnp.where(is0, F32(TOK), F32(0.0))
    end_flag = jnp.where(is0, flag1, F32(1.0))

    def local_state(keys, values, head):
        kept = jnp.exp(-slopes[head] * to_end) * end_flag
        return dot(keys, (kept * values.astype(F32)).astype(BF16), 0, 0)

    loads[0].wait()
    loads[1].wait()
    for i in range(HALF):
        local_other[i] = local_state(
            k_other[:, cols(i)], v_other[:, cols(i)], HALF * (1 - core) + i
        ).astype(BF16)
    state_swap.start()
    loads[4].wait()
    loads[5].wait()
    for i in range(HALF):
        local[i] = local_state(k[own, cols(i)], v[own, cols(i)], HALF * core + i)

    far = lax.rem(z // PER + HALF // 2, HALF)
    near = z // PER
    between = [lax.rem(far + d, HALF) for d in (1, 3)]
    next_door = z + 1 - 2 * lax.rem(z, 2)
    send_order = [far] + between + [near]
    use_order = [near] + between[::-1] + [far]

    def shares_of(i):
        return [next_door] if i is near else [PER * i + j for j in range(PER)]

    def share_copy(phase, other):
        return remote(
            share_out.at[phase, other],
            share_in.at[phase, z],
            share_send.at[phase, other],
            share_recv.at[phase, z],
            at_z(other),
        )

    def share_arrival(phase, other):
        return remote(
            share_out.at[phase, z],
            share_in.at[phase, other],
            share_send.at[phase, other],
            share_recv.at[phase, other],
            at_z(other),
        )

    def back_copy(phase, other):
        return remote(
            back_out.at[phase, other],
            back_in.at[phase, z],
            back_send.at[phase, other],
            back_recv.at[phase, z],
            at_z(other),
        )

    def put_shares(phase, i, value):
        share_out[phase, pl.ds(PER * i, PER)] = value.astype(BF16).reshape(PER, SHARE, HD)

    def send_shares(phase, i, value):
        put_shares(phase, i, value)
        for other in shares_of(i):
            share_copy(phase, other).start()
        if i is near:
            share_in[phase, z] = share_out[phase, z]

    def turn(phase, backward):
        for other in ring[::-1]:
            share_arrival(phase, other).wait_recv()
        order = range(ZN - 1, -1, -1) if backward else range(ZN)
        total = jnp.zeros((SHARE, HD), F32)
        product = jnp.ones((1, HD), F32)
        before, products = {}, {}
        for j in order:
            before[j], products[j] = total, product
            total = total * step_decay[j] + share_in[phase, j].astype(F32)
            product = product * step_decay[j]
        carry_out[phase] = total.astype(BF16)
        carry = remote(
            carry_out.at[phase],
            carry_in.at[phase],
            carry_send.at[phase],
            carry_recv.at[phase],
            below(z) if backward else above(z),
        )
        carry.start()
        carry.wait_recv()
        incoming = carry_in[phase].astype(F32)
        for j in range(ZN):
            back_out[phase, j] = (before[j] + products[j] * incoming).astype(BF16)
        for other in ring:
            back_copy(phase, other).start()
        back_in[phase, z] = back_out[phase, z]
        for other in ring:
            share_copy(phase, other).wait_send()
        carry.wait_send()

    def arrived(phase, i):
        for other in shares_of(i):
            remote(
                back_out.at[phase, z],
                back_in.at[phase, other],
                back_send.at[phase, other],
                back_recv.at[phase, other],
                at_z(other),
            ).wait_recv()
        return state(phase, i)

    def state(phase, i):
        return back_in[phase, pl.ds(PER * i, PER)].reshape(HD, HD)

    state_swap.wait_recv()
    for i in range(HALF):
        put_shares(0, i, local[i] + local_in[i].astype(F32))
    share_in[0, z] = share_out[0, z]
    for other in ring:

        @pl.when(other < z)
        def _():
            share_copy(0, other).start()

    for other in range(1, ZN):

        @pl.when(other > z)
        def _():
            pl.semaphore_wait(answers.at[other], 1)
            share_copy(0, other).start()

    for swap in swaps:
        swap.start()

    share_slope = slopes[HALF * core + z // PER]
    lam2 = jnp.exp(jnp.full((1, HD), -1.0 * PAIR, F32) * share_slope)
    step_decay = [
        lam2 * (carries(y * (2 * ZN) + 2 * j) * carries(y * (2 * ZN) + 2 * j + 1))
        for j in range(ZN)
    ]

    loads[6].wait()
    for i in range(HALF):
        begin = pl.multiple_of(core * WIDE + i * HD, HD)
        gain[:, i * HD : (i + 1) * HD] = gain_flat[pl.ds(begin, HD)].reshape(1, HD)
    token = lax.broadcasted_iota(jnp.int32, (PAIR, HD), 0)
    second = token >= TOK
    token_f = token.astype(F32)
    entry_flag = jnp.where(second, flag0 * flag1, flag0)
    tail_flag = jnp.where(second, 1.0, flag1)
    row = lax.broadcasted_iota(jnp.int32, (PAIR, PAIR), 0)
    column = lax.broadcasted_iota(jnp.int32, (PAIR, PAIR), 1)
    distance = (row - column).astype(F32)
    reach = jnp.where((row >= TOK) & (column < TOK), flag1, 1.0)
    for i in range(HALF):
        entries[i] = jnp.exp(-slope[i] * (token_f + 1.0)) * entry_flag
        tails[i] = jnp.exp(-slope[i] * (PAIR - 1.0 - token_f)) * tail_flag
        table[i] = jnp.where(
            distance >= 0.0, jnp.exp(-slope[i] * jnp.maximum(distance, 0.0)) * reach, 0.0
        )
    for load in loads[7:]:
        load.wait()
    for swap in swaps:
        swap.wait_recv()
    for i in range(HALF):
        weight = (dot(q[:, cols(i)], k[:, cols(i)], 1, 1) * table[i]).astype(BF16)
        weights[i] = weight
        raw[:, cols(i)] = dot(weight, v[:, cols(i)], 1, 0)

    wait_some(answers.at[ZN], 2 - lower_y)
    turn(0, False)
    squares = jnp.zeros((PAIR, HD), F32)
    products = jnp.zeros((PAIR, HD), F32)
    for i in use_order:
        raw_i = raw[:, cols(i)] + dot(q[:, cols(i)], arrived(0, i), 1, 0) * entries[i]
        raw[:, cols(i)] = raw_i
        squares = squares + raw_i * raw_i
        products = products + raw_i * (og[:, cols(i)].astype(F32) * gain[:, cols(i)])

    def token_row(values):
        return jnp.sum(values.T, axis=0, keepdims=True)

    place = lax.broadcasted_iota(jnp.int32, (8, HD), 0)
    slot = 2 * x + core
    sums[slot] = jnp.where(
        place < 4,
        jnp.where(place < 2, token_row(squares[:TOK]), token_row(squares[TOK:])),
        jnp.where(place < 6, token_row(products[:TOK]), token_row(products[TOK:])),
    )
    wait_some(answers.at[ZN + 1], 2 * (XN - 1 - x))
    sum_copies = []
    for index, target in cross:
        copy = remote(
            sums.at[slot], sums.at[slot], sums_send.at[index], sums_recv.at[slot], target
        )
        copy.start()
        sum_copies.append(copy)
    for index, target in cross[::-1]:
        remote(
            sums.at[slot], sums.at[index], sums_send.at[index], sums_recv.at[index], target
        ).wait_recv()
    total = sums[0]
    for j in range(1, 2 * XN):
        total = total + sums[j]
    inverse_rows = lax.rsqrt(total[0:4] / features + EPSILON)
    factor_rows = inverse_rows * inverse_rows * inverse_rows * total[4:8] / features

    def token_columns(rows):
        return jnp.concatenate(
            [jnp.broadcast_to(rows[j : j + 1], (HD, HD)).T for j in (0, 2)], axis=0
        )

    inverse = token_columns(inverse_rows)
    factor = token_columns(factor_rows)

    for i in send_order:
        scaled = og[:, cols(i)].astype(F32) * gain[:, cols(i)]
        grad = (inverse * scaled - factor * raw[:, cols(i)]).astype(BF16)
        og[:, cols(i)] = grad
        query_decayed = (entries[i] * q[:, cols(i)].astype(F32)).astype(BF16)
        send_shares(1, i, dot(query_decayed, grad, 0, 0))

    results = []

    def deliver(source, target):
        j = len(results) // 2
        keep = pltpu.make_async_copy(source.at[own], target.at[:, mine], own_sem.at[j])
        send = remote(
            source.at[other_rows], target.at[:, mine], result_send.at[j], result_recv.at[j], sib
        )
        send.start()
        keep.start()
        results.extend((keep, send))

    for i in range(HALF):
        att[:, cols(i)] = (raw[:, cols(i)] * inverse * gain[:, cols(i)]).astype(BF16)
    deliver(att, att_out)
    for i in range(HALF):
        grad = og[:, cols(i)]
        dscore = (dot(grad, v[:, cols(i)], 1, 1) * table[i]).astype(BF16)
        dq[:, cols(i)] = (
            dot(dscore, k[:, cols(i)], 1, 0) + dot(grad, state(0, i), 1, 1) * entries[i]
        ).astype(BF16)
        dk_part[:, cols(i)] = dot(dscore, q[:, cols(i)], 0, 0)
        dv_part[:, cols(i)] = dot(weights[i], grad, 0, 0)
    deliver(dq, dq_out)

    turn(1, True)

    def finish(j, i, value, target):
        value = value.astype(BF16)
        place_at = pl.ds(pl.multiple_of(core * WIDE + i * HD, HD), HD)
        target[:, place_at] = jnp.where(is0, value[:TOK], value[TOK:])
        last[j, i] = jnp.where(is0, value[TOK:], value[:TOK])
        return remote(
            last.at[j, i], target.at[:, place_at], last_send.at[j, i], last_recv.at[j, i], sib
        )

    finals = []
    for i in use_order:
        grad_state = arrived(1, i)
        for j, (part, operand, side, target) in enumerate(
            ((dk_part, v, 1, dk_out), (dv_part, k, 0, dv_out))
        ):
            copy = finish(
                j,
                i,
                part[:, cols(i)] + dot(operand[:, cols(i)], grad_state, 1, side) * tails[i],
                target,
            )
            copy.start()
            finals.append(copy)

    for swap in swaps + [state_swap]:
        swap.wait_send()
    for copy in sum_copies:
        copy.wait_send()
    for phase in range(2):
        for other in ring:
            back_copy(phase, other).wait_send()
    for copy in results + finals:
        copy.wait()


def place_results(*refs):
    sources, targets, sems = refs[:4], refs[4:8], refs[8]
    copies = [
        pltpu.make_async_copy(src, dst, sems.at[i])
        for i, (src, dst) in enumerate(zip(sources, targets))
    ]
    for copy in copies:
        copy.start()
    for copy in copies:
        copy.wait()


def body(query_rows, key_rows, value_rows, out_grad, slopes, norm_gain, doc_lengths):
    rows, width = query_rows.shape
    features = width * lax.axis_size("tp")
    whole = jax.ShapeDtypeStruct((rows, width), BF16)
    in_hbm = pl.BlockSpec(memory_space=pltpu.HBM)
    in_vmem = pl.BlockSpec(memory_space=pltpu.VMEM)
    dma = pltpu.SemaphoreType.DMA
    pair_bf16 = pltpu.VMEM((PAIR, WIDE), BF16)
    pair_f32 = pltpu.VMEM((PAIR, WIDE), F32)
    shares = pltpu.VMEM((2, ZN, SHARE, HD), BF16)
    carry = pltpu.VMEM((2, SHARE, HD), BF16)
    results = pl.pallas_call(
        functools.partial(kernel, features),
        out_shape=(pltpu.VMEM((rows, width), BF16),) * 4,
        in_specs=[in_hbm] * 7,
        out_specs=(in_vmem,) * 4,
        scratch_shapes=[
            pltpu.SMEM(slopes.shape, F32),
            pltpu.SMEM(doc_lengths.shape, jnp.int32),
            pltpu.VMEM((width,), F32),
            pltpu.VMEM((1, WIDE), F32),
            pair_bf16,
            pair_bf16,
            pair_bf16,
            pair_bf16,
            pltpu.VMEM((TOK, WIDE), BF16),
            pltpu.VMEM((TOK, WIDE), BF16),
            pair_bf16,
            pair_bf16,
            pltpu.VMEM((2, HALF, TOK, HD), BF16),
            pltpu.VMEM((HALF, PAIR, HD), F32),
            pltpu.VMEM((HALF, PAIR, HD), F32),
            pltpu.VMEM((HALF, HD, HD), F32),
            pltpu.VMEM((HALF, HD, HD), BF16),
            pltpu.VMEM((HALF, HD, HD), BF16),
            pltpu.VMEM((HALF, PAIR, PAIR), F32),
            pltpu.VMEM((HALF, PAIR, PAIR), BF16),
            pair_f32,
            pair_f32,
            pair_f32,
            shares,
            shares,
            carry,
            carry,
            shares,
            shares,
            pltpu.VMEM((2 * XN, 8, HD), F32),
            pltpu.SemaphoreType.REGULAR((ZN + 2,)),
            dma((9,)),
            dma((2,)),
            dma((5,)),
            dma((5,)),
            dma((2, ZN)),
            dma((2, ZN)),
            dma((2,)),
            dma((2,)),
            dma((2, ZN)),
            dma((2, ZN)),
            dma((2 * XN,)),
            dma((2 * XN,)),
            dma((2,)),
            dma((2,)),
            dma((2, HALF)),
            dma((2, HALF)),
        ],
        compiler_params=pltpu.CompilerParams(
            collective_id=0, has_side_effects=True, vmem_limit_bytes=48 * 1024 * 1024
        ),
        name="lightning",
    )(
        *(
            pltpu.with_memory_space_constraint(a, pltpu.HBM)
            for a in (slopes, doc_lengths, query_rows, key_rows, value_rows, out_grad, norm_gain)
        )
    )
    return pl.pallas_call(
        place_results,
        out_shape=(whole,) * 4,
        in_specs=[in_vmem] * 4,
        out_specs=(in_hbm,) * 4,
        scratch_shapes=[dma((4,))],
        compiler_params=pltpu.CompilerParams(vmem_limit_bytes=8 * 1024 * 1024),
        name="place",
    )(*(pltpu.with_memory_space_constraint(a, pltpu.VMEM) for a in results))


def solution(mesh):
    spec = P("ctx", "tp")
    in_specs = (spec, spec, spec, spec, P("tp"), P("tp"), P())
    return jax.shard_map(
        body, mesh=mesh, in_specs=in_specs, out_specs=(spec,) * 4, check_vma=False
    )
```

```python
import functools

import jax
import jax.numpy as jnp
from jax import lax
from jax.experimental import pallas as pl
from jax.experimental.pallas import tpu as pltpu
from jax.sharding import PartitionSpec as P

HD = 128
EPSILON = 1e-06
MESH = pl.DeviceIdType.MESH
F32 = jnp.float32
BF16 = jnp.bfloat16
TOK = 128
PAIR = 2 * TOK
HALF = 4
WIDE = HALF * HD
ZN = 8
SHARE = HALF * HD // ZN
PER = ZN // HALF
XN = 4


def dot(a, b, ca, cb):
    return lax.dot_general(a, b, (((ca,), (cb,)), ((), ())), preferred_element_type=F32)


def kernel(
    features,
    slopes_hbm,
    doc_hbm,
    q_hbm,
    k_hbm,
    v_hbm,
    og_hbm,
    gain_hbm,
    att_out,
    dq_out,
    dk_out,
    dv_out,
    slopes,
    doc_lengths,
    gain_flat,
    gain,
    q,
    k,
    v,
    og,
    k_other,
    v_other,
    att,
    dq,
    last,
    entries,
    tails,
    local,
    local_other,
    local_in,
    table,
    weights,
    raw,
    dk_part,
    dv_part,
    share_out,
    share_in,
    carry_out,
    carry_in,
    back_out,
    back_in,
    kept,
    to_end_decay,
    sums,
    answers,
    local_sem,
    own_sem,
    swap_send,
    swap_recv,
    share_send,
    share_recv,
    carry_send,
    carry_recv,
    back_send,
    back_recv,
    sums_send,
    sums_recv,
    result_send,
    result_recv,
    last_send,
    last_recv,
):
    ctx = lax.axis_index("ctx")
    x = lax.axis_index("tp")
    rows_y = lax.axis_size("ctx") // (2 * ZN)
    core = lax.rem(ctx, 2)
    z = lax.rem(ctx // 2, ZN)
    y = ctx // (2 * ZN)

    def device(dx, y_at, z_at, core_at):
        return (y_at * (2 * ZN) + z_at * 2 + core_at, lax.rem(x + dx, XN))

    sib = device(0, y, z, 1 - core)
    ring = [lax.rem(z + d, ZN) for d in (4, 3, 5, 2, 6, 1, 7)]
    heads_of = [(2, 1), (2, 0), (1, 1), (3, 1), (1, 0), (3, 0), (0, 1)]
    cross = [
        (2 * lax.rem(x + dx, XN) + lax.rem(core + dc, 2), device(dx, y, z, lax.rem(core + dc, 2)))
        for dx, dc in heads_of
    ]

    next_y, last_y = lax.rem(y + 1, rows_y), lax.rem(y + rows_y - 1, rows_y)

    def at_z(other):
        return device(0, y, other, core)

    def above(other):
        return device(0, next_y, other, core)

    def below(other):
        return device(0, last_y, other, core)


    mine = pl.ds(pl.multiple_of(core * WIDE, WIDE), WIDE)
    theirs = pl.ds(pl.multiple_of((1 - core) * WIDE, WIDE), WIDE)
    own = pl.ds(pl.multiple_of(core * TOK, TOK), TOK)
    other_rows = pl.ds(pl.multiple_of((1 - core) * TOK, TOK), TOK)

    loads = [
        pltpu.make_async_copy(src, dst, local_sem.at[i])
        for i, (src, dst) in enumerate(
            (
                (k_hbm.at[:, theirs], k_other),
                (v_hbm.at[:, theirs], v_other),
                (slopes_hbm, slopes),
                (doc_hbm, doc_lengths),
                (k_hbm.at[:, mine], k.at[own]),
                (v_hbm.at[:, mine], v.at[own]),
                (gain_hbm, gain_flat),
                (q_hbm.at[:, mine], q.at[own]),
                (og_hbm.at[:, mine], og.at[own]),
            )
        )
    ]
    for load in loads[:4]:
        load.start()

    barrier = pltpu.get_barrier_semaphore()
    along_z = [(other, at_z(other)) for other in ring]
    along_y = [(next_y, above(z)), (last_y, below(z))]
    along_x = [(index // 2, target) for index, target in cross[:-1]]

    def signal_if(condition, semaphore, target):
        @pl.when(condition)
        def _():
            pl.semaphore_signal(semaphore, 1, device_id=target, device_id_type=MESH)

    pl.semaphore_signal(barrier, 1, device_id=sib, device_id_type=MESH)
    for here, partners in ((z, along_z), (y, along_y), (x, along_x)):
        for other, target in partners:
            signal_if(other > here, barrier, target)
    lower_y = (next_y < y).astype(jnp.int32) + (last_y < y).astype(jnp.int32)
    greetings = 1 + z + lower_y + 2 * x

    def wait_some(semaphore, count):
        @pl.when(count > 0)
        def _():
            pl.semaphore_wait(semaphore, count)

    def answer():
        for other, target in along_z:
            signal_if(other < z, answers.at[z], target)
        for axis, here, partners in ((ZN, y, along_y), (ZN + 1, x, along_x)):
            for other, target in partners:
                signal_if(other < here, answers.at[axis], target)

    for load in loads[4:]:
        load.start()
    pl.semaphore_wait(barrier, greetings)
    answer()

    def remote(src, dst, send, recv, target):
        return pltpu.make_async_remote_copy(
            src_ref=src,
            dst_ref=dst,
            send_sem=send,
            recv_sem=recv,
            device_id=target,
            device_id_type=MESH,
        )

    swaps = [
        remote(src, dst.at[own], swap_send.at[i], swap_recv.at[i], sib)
        for i, (src, dst) in enumerate(
            ((k_other, k), (v_other, v), (q_hbm.at[:, theirs], q), (og_hbm.at[:, theirs], og))
        )
    ]
    state_swap = remote(local_other, local_in, swap_send.at[4], swap_recv.at[4], sib)

    for load in loads[2:4]:
        load.wait()

    starts = [jnp.int32(0)]
    for j in range(doc_lengths.shape[0] - 1):
        starts.append(starts[-1] + doc_lengths[j])

    def carries(block):
        hit = starts[0] == block
        for start in starts[1:]:
            hit = hit | (start == block)
        return jnp.where(hit, F32(0.0), F32(1.0))

    flag0 = carries(y * (2 * ZN) + 2 * z)
    flag1 = carries(y * (2 * ZN) + 2 * z + 1)
    slope = [slopes[HALF * core + i] for i in range(HALF)]
    def cols(i):
        return pl.ds(pl.multiple_of(i * HD, HD), HD)

    is0 = core == 0
    to_end = (TOK - 1.0) - lax.broadcasted_iota(jnp.int32, (TOK, HD), 0).astype(F32)
    to_end = to_end + jnp.where(is0, F32(TOK), F32(0.0))
    end_flag = jnp.where(is0, flag1, F32(1.0))

    def local_state(keys, values, head):
        kept = jnp.exp(-slopes[head] * to_end) * end_flag
        return dot(keys, (kept * values.astype(F32)).astype(BF16), 0, 0)

    loads[0].wait()
    loads[1].wait()
    for i in range(HALF):
        local_other[i] = local_state(
            k_other[:, cols(i)], v_other[:, cols(i)], HALF * (1 - core) + i
        ).astype(BF16)
    state_swap.start()
    loads[4].wait()
    loads[5].wait()
    for i in range(HALF):
        local[i] = local_state(k[own, cols(i)], v[own, cols(i)], HALF * core + i)

    far = lax.rem(z // PER + HALF // 2, HALF)
    near = z // PER
    between = [lax.rem(far + d, HALF) for d in (1, 3)]
    next_door = z + 1 - 2 * lax.rem(z, 2)
    send_order = [far] + between + [near]
    use_order = [near] + between[::-1] + [far]

    def shares_of(i):
        return [next_door] if i is near else [PER * i + j for j in range(PER)]

    def share_copy(phase, other):
        return remote(
            share_out.at[phase, other],
            share_in.at[phase, z],
            share_send.at[phase, other],
            share_recv.at[phase, z],
            at_z(other),
        )

    def share_arrival(phase, other):
        return remote(
            share_out.at[phase, z],
            share_in.at[phase, other],
            share_send.at[phase, other],
            share_recv.at[phase, other],
            at_z(other),
        )

    def back_copy(phase, other):
        return remote(
            back_out.at[phase, other],
            back_in.at[phase, z],
            back_send.at[phase, other],
            back_recv.at[phase, z],
            at_z(other),
        )

    def put_shares(phase, i, value):
        share_out[phase, pl.ds(PER * i, PER)] = value.astype(BF16).reshape(PER, SHARE, HD)

    def send_shares(phase, i, value):
        put_shares(phase, i, value)
        for other in shares_of(i):
            share_copy(phase, other).start()
        if i is near:
            share_in[phase, z] = share_out[phase, z]

    def turn(phase, backward):
        total = share_in[phase, z].astype(F32) * to_end_decay[phase, z]
        for other in ring[::-1]:
            share_arrival(phase, other).wait_recv()
            total = total + share_in[phase, other].astype(F32) * to_end_decay[phase, other]
        carry_out[phase] = total.astype(BF16)
        carry = remote(
            carry_out.at[phase],
            carry_in.at[phase],
            carry_send.at[phase],
            carry_recv.at[phase],
            below(z) if backward else above(z),
        )
        carry.start()
        inside = jnp.zeros((SHARE, HD), F32)
        for j in range(ZN - 1, -1, -1) if backward else range(ZN):
            kept[j] = inside
            inside = inside * step_decay[j] + share_in[phase, j].astype(F32)
        carry.wait_recv()
        incoming = carry_in[phase].astype(F32)
        if backward:
            for other in range(ZN):
                back_out[phase, other] = (
                    kept[other] + to_end_decay[2 + phase, other] * incoming
                ).astype(BF16)

                @pl.when(other != z)
                def _():
                    back_copy(phase, other).start()

        else:
            for other in ring:
                back_out[phase, other] = (
                    kept[other] + to_end_decay[2 + phase, other] * incoming
                ).astype(BF16)
                back_copy(phase, other).start()
        back_in[phase, z] = (kept[z] + to_end_decay[2 + phase, z] * incoming).astype(BF16)
        for other in ring:
            share_copy(phase, other).wait_send()
        carry.wait_send()

    def arrived(phase, i):
        for other in shares_of(i):
            remote(
                back_out.at[phase, z],
                back_in.at[phase, other],
                back_send.at[phase, other],
                back_recv.at[phase, other],
                at_z(other),
            ).wait_recv()
        return state(phase, i)

    def state(phase, i):
        return back_in[phase, pl.ds(PER * i, PER)].reshape(HD, HD)

    state_swap.wait_recv()
    for i in range(HALF):
        put_shares(0, i, local[i] + local_in[i].astype(F32))
    share_in[0, z] = share_out[0, z]
    for other in ring:

        @pl.when(other < z)
        def _():
            share_copy(0, other).start()

    for other in range(1, ZN):

        @pl.when(other > z)
        def _():
            pl.semaphore_wait(answers.at[other], 1)
            share_copy(0, other).start()

    for swap in swaps:
        swap.start()

    share_slope = slopes[HALF * core + z // PER]
    lam2 = jnp.exp(jnp.full((1, HD), -1.0 * PAIR, F32) * share_slope)
    step_decay = [
        lam2 * (carries(y * (2 * ZN) + 2 * j) * carries(y * (2 * ZN) + 2 * j + 1))
        for j in range(ZN)
    ]

    after, ahead = jnp.ones((1, HD), F32), jnp.ones((1, HD), F32)
    for j in range(ZN):
        to_end_decay[1, j] = after
        to_end_decay[2, j] = after
        to_end_decay[0, ZN - 1 - j] = ahead
        to_end_decay[3, ZN - 1 - j] = ahead
        after = after * step_decay[j]
        ahead = ahead * step_decay[ZN - 1 - j]

    loads[6].wait()
    for i in range(HALF):
        begin = pl.multiple_of(core * WIDE + i * HD, HD)
        gain[:, i * HD : (i + 1) * HD] = gain_flat[pl.ds(begin, HD)].reshape(1, HD)
    token = lax.broadcasted_iota(jnp.int32, (PAIR, HD), 0)
    second = token >= TOK
    token_f = token.astype(F32)
    entry_flag = jnp.where(second, flag0 * flag1, flag0)
    tail_flag = jnp.where(second, 1.0, flag1)
    row = lax.broadcasted_iota(jnp.int32, (PAIR, PAIR), 0)
    column = lax.broadcasted_iota(jnp.int32, (PAIR, PAIR), 1)
    distance = (row - column).astype(F32)
    reach = jnp.where((row >= TOK) & (column < TOK), flag1, 1.0)
    for i in range(HALF):
        entries[i] = jnp.exp(-slope[i] * (token_f + 1.0)) * entry_flag
        tails[i] = jnp.exp(-slope[i] * (PAIR - 1.0 - token_f)) * tail_flag
        table[i] = jnp.where(
            distance >= 0.0, jnp.exp(-slope[i] * jnp.maximum(distance, 0.0)) * reach, 0.0
        )
    for load in loads[7:]:
        load.wait()
    for swap in swaps:
        swap.wait_recv()
    for i in range(HALF):
        weight = (dot(q[:, cols(i)], k[:, cols(i)], 1, 1) * table[i]).astype(BF16)
        weights[i] = weight
        raw[:, cols(i)] = dot(weight, v[:, cols(i)], 1, 0)

    wait_some(answers.at[ZN], 2 - lower_y)
    turn(0, False)
    squares = jnp.zeros((PAIR, HD), F32)
    products = jnp.zeros((PAIR, HD), F32)
    for i in use_order:
        raw_i = raw[:, cols(i)] + dot(q[:, cols(i)], arrived(0, i), 1, 0) * entries[i]
        raw[:, cols(i)] = raw_i
        squares = squares + raw_i * raw_i
        products = products + raw_i * (og[:, cols(i)].astype(F32) * gain[:, cols(i)])

    def token_row(values):
        return jnp.sum(values.T, axis=0, keepdims=True)

    place = lax.broadcasted_iota(jnp.int32, (8, HD), 0)
    slot = 2 * x + core
    sums[slot] = jnp.where(
        place < 4,
        jnp.where(place < 2, token_row(squares[:TOK]), token_row(squares[TOK:])),
        jnp.where(place < 6, token_row(products[:TOK]), token_row(products[TOK:])),
    )
    wait_some(answers.at[ZN + 1], 2 * (XN - 1 - x))
    sum_copies = []
    for index, target in cross:
        copy = remote(
            sums.at[slot], sums.at[slot], sums_send.at[index], sums_recv.at[slot], target
        )
        copy.start()
        sum_copies.append(copy)
    for index, target in cross[::-1]:
        remote(
            sums.at[slot], sums.at[index], sums_send.at[index], sums_recv.at[index], target
        ).wait_recv()
    total = sums[0]
    for j in range(1, 2 * XN):
        total = total + sums[j]
    inverse_rows = lax.rsqrt(total[0:4] / features + EPSILON)
    factor_rows = inverse_rows * inverse_rows * inverse_rows * total[4:8] / features

    def token_columns(rows):
        return jnp.concatenate(
            [jnp.broadcast_to(rows[j : j + 1], (HD, HD)).T for j in (0, 2)], axis=0
        )

    inverse = token_columns(inverse_rows)
    factor = token_columns(factor_rows)

    for i in send_order:
        scaled = og[:, cols(i)].astype(F32) * gain[:, cols(i)]
        grad = (inverse * scaled - factor * raw[:, cols(i)]).astype(BF16)
        og[:, cols(i)] = grad
        query_decayed = (entries[i] * q[:, cols(i)].astype(F32)).astype(BF16)
        send_shares(1, i, dot(query_decayed, grad, 0, 0))

    results = []

    def deliver(source, target):
        j = len(results) // 2
        keep = pltpu.make_async_copy(source.at[own], target.at[:, mine], own_sem.at[j])
        send = remote(
            source.at[other_rows], target.at[:, mine], result_send.at[j], result_recv.at[j], sib
        )
        send.start()
        keep.start()
        results.extend((keep, send))

    for i in range(HALF):
        att[:, cols(i)] = (raw[:, cols(i)] * inverse * gain[:, cols(i)]).astype(BF16)
    deliver(att, att_out)
    for i in range(HALF):
        grad = og[:, cols(i)]
        dscore = (dot(grad, v[:, cols(i)], 1, 1) * table[i]).astype(BF16)
        dq[:, cols(i)] = (
            dot(dscore, k[:, cols(i)], 1, 0) + dot(grad, state(0, i), 1, 1) * entries[i]
        ).astype(BF16)
        dk_part[:, cols(i)] = dot(dscore, q[:, cols(i)], 0, 0)
        dv_part[:, cols(i)] = dot(weights[i], grad, 0, 0)
    deliver(dq, dq_out)

    turn(1, True)

    def finish(j, i, value, target):
        value = value.astype(BF16)
        place_at = pl.ds(pl.multiple_of(core * WIDE + i * HD, HD), HD)
        target[:, place_at] = jnp.where(is0, value[:TOK], value[TOK:])
        last[j, i] = jnp.where(is0, value[TOK:], value[:TOK])
        return remote(
            last.at[j, i], target.at[:, place_at], last_send.at[j, i], last_recv.at[j, i], sib
        )

    finals = []
    for i in use_order:
        grad_state = arrived(1, i)
        for j, (part, operand, side, target) in enumerate(
            ((dk_part, v, 1, dk_out), (dv_part, k, 0, dv_out))
        ):
            copy = finish(
                j,
                i,
                part[:, cols(i)] + dot(operand[:, cols(i)], grad_state, 1, side) * tails[i],
                target,
            )
            copy.start()
            finals.append(copy)

    for swap in swaps + [state_swap]:
        swap.wait_send()
    for copy in sum_copies:
        copy.wait_send()
    for phase in range(2):
        for other in ring:
            back_copy(phase, other).wait_send()
    for copy in results + finals:
        copy.wait()


def place_results(*refs):
    sources, targets, sems = refs[:4], refs[4:8], refs[8]
    copies = [
        pltpu.make_async_copy(src, dst, sems.at[i])
        for i, (src, dst) in enumerate(zip(sources, targets))
    ]
    for copy in copies:
        copy.start()
    for copy in copies:
        copy.wait()


def body(query_rows, key_rows, value_rows, out_grad, slopes, norm_gain, doc_lengths):
    rows, width = query_rows.shape
    features = width * lax.axis_size("tp")
    whole = jax.ShapeDtypeStruct((rows, width), BF16)
    in_hbm = pl.BlockSpec(memory_space=pltpu.HBM)
    in_vmem = pl.BlockSpec(memory_space=pltpu.VMEM)
    dma = pltpu.SemaphoreType.DMA
    pair_bf16 = pltpu.VMEM((PAIR, WIDE), BF16)
    pair_f32 = pltpu.VMEM((PAIR, WIDE), F32)
    shares = pltpu.VMEM((2, ZN, SHARE, HD), BF16)
    carry = pltpu.VMEM((2, SHARE, HD), BF16)
    results = pl.pallas_call(
        functools.partial(kernel, features),
        out_shape=(pltpu.VMEM((rows, width), BF16),) * 4,
        in_specs=[in_hbm] * 7,
        out_specs=(in_vmem,) * 4,
        scratch_shapes=[
            pltpu.SMEM(slopes.shape, F32),
            pltpu.SMEM(doc_lengths.shape, jnp.int32),
            pltpu.VMEM((width,), F32),
            pltpu.VMEM((1, WIDE), F32),
            pair_bf16,
            pair_bf16,
            pair_bf16,
            pair_bf16,
            pltpu.VMEM((TOK, WIDE), BF16),
            pltpu.VMEM((TOK, WIDE), BF16),
            pair_bf16,
            pair_bf16,
            pltpu.VMEM((2, HALF, TOK, HD), BF16),
            pltpu.VMEM((HALF, PAIR, HD), F32),
            pltpu.VMEM((HALF, PAIR, HD), F32),
            pltpu.VMEM((HALF, HD, HD), F32),
            pltpu.VMEM((HALF, HD, HD), BF16),
            pltpu.VMEM((HALF, HD, HD), BF16),
            pltpu.VMEM((HALF, PAIR, PAIR), F32),
            pltpu.VMEM((HALF, PAIR, PAIR), BF16),
            pair_f32,
            pair_f32,
            pair_f32,
            shares,
            shares,
            carry,
            carry,
            shares,
            shares,
            pltpu.VMEM((ZN, SHARE, HD), F32),
            pltpu.VMEM((4, ZN, 1, HD), F32),
            pltpu.VMEM((2 * XN, 8, HD), F32),
            pltpu.SemaphoreType.REGULAR((ZN + 2,)),
            dma((9,)),
            dma((2,)),
            dma((5,)),
            dma((5,)),
            dma((2, ZN)),
            dma((2, ZN)),
            dma((2,)),
            dma((2,)),
            dma((2, ZN)),
            dma((2, ZN)),
            dma((2 * XN,)),
            dma((2 * XN,)),
            dma((2,)),
            dma((2,)),
            dma((2, HALF)),
            dma((2, HALF)),
        ],
        compiler_params=pltpu.CompilerParams(
            collective_id=0, has_side_effects=True, vmem_limit_bytes=48 * 1024 * 1024
        ),
        name="lightning",
    )(
        *(
            pltpu.with_memory_space_constraint(a, pltpu.HBM)
            for a in (slopes, doc_lengths, query_rows, key_rows, value_rows, out_grad, norm_gain)
        )
    )
    return pl.pallas_call(
        place_results,
        out_shape=(whole,) * 4,
        in_specs=[in_vmem] * 4,
        out_specs=(in_hbm,) * 4,
        scratch_shapes=[dma((4,))],
        compiler_params=pltpu.CompilerParams(vmem_limit_bytes=8 * 1024 * 1024),
        name="place",
    )(*(pltpu.with_memory_space_constraint(a, pltpu.VMEM) for a in results))


def solution(mesh):
    spec = P("ctx", "tp")
    in_specs = (spec, spec, spec, spec, P("tp"), P("tp"), P())
    return jax.shard_map(
        body, mesh=mesh, in_specs=in_specs, out_specs=(spec,) * 4, check_vma=False
    )
```

```python
import functools

import jax
import jax.numpy as jnp
from jax import lax
from jax.experimental import pallas as pl
from jax.experimental.pallas import tpu as pltpu
from jax.sharding import PartitionSpec as P

HD = 128
EPSILON = 1e-06
MESH = pl.DeviceIdType.MESH
F32 = jnp.float32
BF16 = jnp.bfloat16
TOK = 128
PAIR = 2 * TOK
HALF = 4
WIDE = HALF * HD
ZN = 8
SHARE = HALF * HD // ZN
PER = ZN // HALF
XN = 4


def dot(a, b, ca, cb):
    return lax.dot_general(a, b, (((ca,), (cb,)), ((), ())), preferred_element_type=F32)


def kernel(
    features,
    slopes_hbm,
    doc_hbm,
    q_hbm,
    k_hbm,
    v_hbm,
    og_hbm,
    gain_hbm,
    att_out,
    dq_out,
    dk_out,
    dv_out,
    slopes,
    doc_lengths,
    gain_flat,
    gain,
    q,
    k,
    v,
    og,
    k_other,
    v_other,
    att,
    dq,
    last,
    entries,
    tails,
    local,
    local_other,
    local_in,
    table,
    weights,
    raw,
    dk_part,
    dv_part,
    share_out,
    share_in,
    carry_out,
    carry_in,
    back_out,
    back_in,
    kept,
    to_end_decay,
    early_in,
    sums,
    answers,
    early_send,
    early_recv,
    local_sem,
    own_sem,
    swap_send,
    swap_recv,
    share_send,
    share_recv,
    carry_send,
    carry_recv,
    back_send,
    back_recv,
    sums_send,
    sums_recv,
    result_send,
    result_recv,
    last_send,
    last_recv,
):
    ctx = lax.axis_index("ctx")
    x = lax.axis_index("tp")
    rows_y = lax.axis_size("ctx") // (2 * ZN)
    core = lax.rem(ctx, 2)
    z = lax.rem(ctx // 2, ZN)
    y = ctx // (2 * ZN)

    def device(dx, y_at, z_at, core_at):
        return (y_at * (2 * ZN) + z_at * 2 + core_at, lax.rem(x + dx, XN))

    sib = device(0, y, z, 1 - core)
    ring = [lax.rem(z + d, ZN) for d in (4, 3, 5, 2, 6, 1, 7)]
    heads_of = [(2, 1), (2, 0), (1, 1), (3, 1), (1, 0), (3, 0), (0, 1)]
    cross = [
        (2 * lax.rem(x + dx, XN) + lax.rem(core + dc, 2), device(dx, y, z, lax.rem(core + dc, 2)))
        for dx, dc in heads_of
    ]

    next_y, last_y = lax.rem(y + 1, rows_y), lax.rem(y + rows_y - 1, rows_y)

    def at_z(other):
        return device(0, y, other, core)

    def above(other):
        return device(0, next_y, other, core)

    def below(other):
        return device(0, last_y, other, core)


    mine = pl.ds(pl.multiple_of(core * WIDE, WIDE), WIDE)
    theirs = pl.ds(pl.multiple_of((1 - core) * WIDE, WIDE), WIDE)
    own = pl.ds(pl.multiple_of(core * TOK, TOK), TOK)
    other_rows = pl.ds(pl.multiple_of((1 - core) * TOK, TOK), TOK)

    loads = [
        pltpu.make_async_copy(src, dst, local_sem.at[i])
        for i, (src, dst) in enumerate(
            (
                (k_hbm.at[:, theirs], k_other),
                (v_hbm.at[:, theirs], v_other),
                (slopes_hbm, slopes),
                (doc_hbm, doc_lengths),
                (k_hbm.at[:, mine], k.at[own]),
                (v_hbm.at[:, mine], v.at[own]),
                (gain_hbm, gain_flat),
                (q_hbm.at[:, mine], q.at[own]),
                (og_hbm.at[:, mine], og.at[own]),
            )
        )
    ]
    for load in loads[:4]:
        load.start()

    barrier = pltpu.get_barrier_semaphore()
    along_z = [(other, at_z(other)) for other in ring]
    along_y = [(next_y, above(z)), (last_y, below(z))]
    along_x = [(index // 2, target) for index, target in cross[:-1]]

    def signal_if(condition, semaphore, target):
        @pl.when(condition)
        def _():
            pl.semaphore_signal(semaphore, 1, device_id=target, device_id_type=MESH)

    pl.semaphore_signal(barrier, 1, device_id=sib, device_id_type=MESH)
    for here, partners in ((z, along_z), (y, along_y), (x, along_x)):
        for other, target in partners:
            signal_if(other > here, barrier, target)
    for other, _ in along_z:
        signal_if((z == 0) & (other > 0), barrier, above(other))
    lower_y = (next_y < y).astype(jnp.int32) + (last_y < y).astype(jnp.int32)
    greetings = 1 + z + lower_y + 2 * x + (z > 0).astype(jnp.int32)

    def wait_some(semaphore, count):
        @pl.when(count > 0)
        def _():
            pl.semaphore_wait(semaphore, count)

    def answer():
        for other, target in along_z:
            signal_if(other < z, answers.at[z], target)
        for axis, here, partners in ((ZN, y, along_y), (ZN + 1, x, along_x)):
            for other, target in partners:
                signal_if(other < here, answers.at[axis], target)

    for load in loads[4:]:
        load.start()
    pl.semaphore_wait(barrier, greetings)
    answer()

    def remote(src, dst, send, recv, target):
        return pltpu.make_async_remote_copy(
            src_ref=src,
            dst_ref=dst,
            send_sem=send,
            recv_sem=recv,
            device_id=target,
            device_id_type=MESH,
        )

    swaps = [
        remote(src, dst.at[own], swap_send.at[i], swap_recv.at[i], sib)
        for i, (src, dst) in enumerate(
            ((k_other, k), (v_other, v), (q_hbm.at[:, theirs], q), (og_hbm.at[:, theirs], og))
        )
    ]
    state_swap = remote(local_other, local_in, swap_send.at[4], swap_recv.at[4], sib)

    for load in loads[2:4]:
        load.wait()

    starts = [jnp.int32(0)]
    for j in range(doc_lengths.shape[0] - 1):
        starts.append(starts[-1] + doc_lengths[j])

    def carries(block):
        hit = starts[0] == block
        for start in starts[1:]:
            hit = hit | (start == block)
        return jnp.where(hit, F32(0.0), F32(1.0))

    flag0 = carries(y * (2 * ZN) + 2 * z)
    flag1 = carries(y * (2 * ZN) + 2 * z + 1)
    slope = [slopes[HALF * core + i] for i in range(HALF)]
    def cols(i):
        return pl.ds(pl.multiple_of(i * HD, HD), HD)

    is0 = core == 0
    to_end = (TOK - 1.0) - lax.broadcasted_iota(jnp.int32, (TOK, HD), 0).astype(F32)
    to_end = to_end + jnp.where(is0, F32(TOK), F32(0.0))
    end_flag = jnp.where(is0, flag1, F32(1.0))

    def local_state(keys, values, head):
        kept = jnp.exp(-slopes[head] * to_end) * end_flag
        return dot(keys, (kept * values.astype(F32)).astype(BF16), 0, 0)

    loads[0].wait()
    loads[1].wait()
    for i in range(HALF):
        local_other[i] = local_state(
            k_other[:, cols(i)], v_other[:, cols(i)], HALF * (1 - core) + i
        ).astype(BF16)
    state_swap.start()
    loads[4].wait()
    loads[5].wait()
    for i in range(HALF):
        local[i] = local_state(k[own, cols(i)], v[own, cols(i)], HALF * core + i)

    far = lax.rem(z // PER + HALF // 2, HALF)
    near = z // PER
    between = [lax.rem(far + d, HALF) for d in (1, 3)]
    next_door = z + 1 - 2 * lax.rem(z, 2)
    send_order = [far] + between + [near]
    use_order = [near] + between[::-1] + [far]

    def shares_of(i):
        return [next_door] if i is near else [PER * i + j for j in range(PER)]

    def share_copy(phase, other):
        return remote(
            share_out.at[phase, other],
            share_in.at[phase, z],
            share_send.at[phase, other],
            share_recv.at[phase, z],
            at_z(other),
        )

    def share_arrival(phase, other):
        return remote(
            share_out.at[phase, z],
            share_in.at[phase, other],
            share_send.at[phase, other],
            share_recv.at[phase, other],
            at_z(other),
        )

    def back_copy(phase, other):
        return remote(
            back_out.at[phase, other],
            back_in.at[phase, z],
            back_send.at[phase, other],
            back_recv.at[phase, z],
            at_z(other),
        )

    def put_shares(phase, i, value):
        share_out[phase, pl.ds(PER * i, PER)] = value.astype(BF16).reshape(PER, SHARE, HD)

    def send_shares(phase, i, value):
        put_shares(phase, i, value)
        for other in shares_of(i):
            share_copy(phase, other).start()
        if i is near:
            share_in[phase, z] = share_out[phase, z]

    def early_copy():
        return remote(
            carry_out.at[1], early_in.at[z], early_send.at[0], early_recv.at[z], below(0)
        )

    def add_early(i):
        @pl.when(z == 0)
        def _():
            decay = jnp.exp(
                jnp.full((1, HD), -1.0 * PAIR * (ZN - 1), F32) * slopes[HALF * core + i]
            )
            decay = decay * row_flag
            for share in shares_of(i):
                remote(
                    carry_out.at[1],
                    early_in.at[share],
                    early_send.at[0],
                    early_recv.at[share],
                    sib,
                ).wait_recv()
                back_in[1, share] = (
                    back_in[1, share].astype(F32) + decay * early_in[share].astype(F32)
                ).astype(BF16)

    def turn(phase, backward):
        total = share_in[phase, z].astype(F32) * to_end_decay[phase, z]
        for other in ring[::-1]:
            share_arrival(phase, other).wait_recv()
            total = total + share_in[phase, other].astype(F32) * to_end_decay[phase, other]
        carry_out[phase] = total.astype(BF16)
        carry = remote(
            carry_out.at[phase],
            carry_in.at[phase],
            carry_send.at[phase],
            carry_recv.at[phase],
            below(z) if backward else above(z),
        )
        carry.start()
        inside = jnp.zeros((SHARE, HD), F32)
        for j in range(ZN - 1, -1, -1) if backward else range(ZN):
            kept[j] = inside
            inside = inside * step_decay[j] + share_in[phase, j].astype(F32)
        if backward:
            back_out[1, 0] = kept[0].astype(BF16)

            @pl.when(z != 0)
            def _():
                early_copy().start()
                back_copy(1, 0).start()

        carry.wait_recv()
        incoming = carry_in[phase].astype(F32)
        if backward:
            for other in range(1, ZN):
                back_out[phase, other] = (
                    kept[other] + to_end_decay[2 + phase, other] * incoming
                ).astype(BF16)

                @pl.when(other != z)
                def _():
                    back_copy(phase, other).start()

        else:
            for other in ring:
                back_out[phase, other] = (
                    kept[other] + to_end_decay[2 + phase, other] * incoming
                ).astype(BF16)
                back_copy(phase, other).start()
        back_in[phase, z] = (kept[z] + to_end_decay[2 + phase, z] * incoming).astype(BF16)
        for other in ring:
            share_copy(phase, other).wait_send()
        carry.wait_send()
        if backward:

            @pl.when(z != 0)
            def _():
                early_copy().wait_send()

    def arrived(phase, i):
        for other in shares_of(i):
            remote(
                back_out.at[phase, z],
                back_in.at[phase, other],
                back_send.at[phase, other],
                back_recv.at[phase, other],
                at_z(other),
            ).wait_recv()
        return state(phase, i)

    def state(phase, i):
        return back_in[phase, pl.ds(PER * i, PER)].reshape(HD, HD)

    state_swap.wait_recv()
    for i in range(HALF):
        put_shares(0, i, local[i] + local_in[i].astype(F32))
    share_in[0, z] = share_out[0, z]
    for other in ring:

        @pl.when(other < z)
        def _():
            share_copy(0, other).start()

    for other in range(1, ZN):

        @pl.when(other > z)
        def _():
            pl.semaphore_wait(answers.at[other], 1)
            share_copy(0, other).start()

    for swap in swaps:
        swap.start()

    share_slope = slopes[HALF * core + z // PER]
    lam2 = jnp.exp(jnp.full((1, HD), -1.0 * PAIR, F32) * share_slope)
    row_flags = [
        carries(y * (2 * ZN) + 2 * j) * carries(y * (2 * ZN) + 2 * j + 1) for j in range(ZN)
    ]
    step_decay = [lam2 * flag for flag in row_flags]
    row_flag = row_flags[1]
    for j in range(2, ZN):
        row_flag = row_flag * row_flags[j]

    after, ahead = jnp.ones((1, HD), F32), jnp.ones((1, HD), F32)
    for j in range(ZN):
        to_end_decay[1, j] = after
        to_end_decay[2, j] = after
        to_end_decay[0, ZN - 1 - j] = ahead
        to_end_decay[3, ZN - 1 - j] = ahead
        after = after * step_decay[j]
        ahead = ahead * step_decay[ZN - 1 - j]

    loads[6].wait()
    for i in range(HALF):
        begin = pl.multiple_of(core * WIDE + i * HD, HD)
        gain[:, i * HD : (i + 1) * HD] = gain_flat[pl.ds(begin, HD)].reshape(1, HD)
    token = lax.broadcasted_iota(jnp.int32, (PAIR, HD), 0)
    second = token >= TOK
    token_f = token.astype(F32)
    entry_flag = jnp.where(second, flag0 * flag1, flag0)
    tail_flag = jnp.where(second, 1.0, flag1)
    row = lax.broadcasted_iota(jnp.int32, (PAIR, PAIR), 0)
    column = lax.broadcasted_iota(jnp.int32, (PAIR, PAIR), 1)
    distance = (row - column).astype(F32)
    reach = jnp.where((row >= TOK) & (column < TOK), flag1, 1.0)
    for i in range(HALF):
        entries[i] = jnp.exp(-slope[i] * (token_f + 1.0)) * entry_flag
        tails[i] = jnp.exp(-slope[i] * (PAIR - 1.0 - token_f)) * tail_flag
        table[i] = jnp.where(
            distance >= 0.0, jnp.exp(-slope[i] * jnp.maximum(distance, 0.0)) * reach, 0.0
        )
    for load in loads[7:]:
        load.wait()
    for swap in swaps:
        swap.wait_recv()
    for i in range(HALF):
        weight = (dot(q[:, cols(i)], k[:, cols(i)], 1, 1) * table[i]).astype(BF16)
        weights[i] = weight
        raw[:, cols(i)] = dot(weight, v[:, cols(i)], 1, 0)

    wait_some(answers.at[ZN], 2 - lower_y)
    turn(0, False)
    squares = jnp.zeros((PAIR, HD), F32)
    products = jnp.zeros((PAIR, HD), F32)
    for i in use_order:
        raw_i = raw[:, cols(i)] + dot(q[:, cols(i)], arrived(0, i), 1, 0) * entries[i]
        raw[:, cols(i)] = raw_i
        squares = squares + raw_i * raw_i
        products = products + raw_i * (og[:, cols(i)].astype(F32) * gain[:, cols(i)])

    def token_row(values):
        return jnp.sum(values.T, axis=0, keepdims=True)

    place = lax.broadcasted_iota(jnp.int32, (8, HD), 0)
    slot = 2 * x + core
    sums[slot] = jnp.where(
        place < 4,
        jnp.where(place < 2, token_row(squares[:TOK]), token_row(squares[TOK:])),
        jnp.where(place < 6, token_row(products[:TOK]), token_row(products[TOK:])),
    )
    wait_some(answers.at[ZN + 1], 2 * (XN - 1 - x))
    sum_copies = []
    for index, target in cross:
        copy = remote(
            sums.at[slot], sums.at[slot], sums_send.at[index], sums_recv.at[slot], target
        )
        copy.start()
        sum_copies.append(copy)
    for index, target in cross[::-1]:
        remote(
            sums.at[slot], sums.at[index], sums_send.at[index], sums_recv.at[index], target
        ).wait_recv()
    total = sums[0]
    for j in range(1, 2 * XN):
        total = total + sums[j]
    inverse_rows = lax.rsqrt(total[0:4] / features + EPSILON)
    factor_rows = inverse_rows * inverse_rows * inverse_rows * total[4:8] / features

    def token_columns(rows):
        return jnp.concatenate(
            [jnp.broadcast_to(rows[j : j + 1], (HD, HD)).T for j in (0, 2)], axis=0
        )

    inverse = token_columns(inverse_rows)
    factor = token_columns(factor_rows)

    for i in send_order:
        scaled = og[:, cols(i)].astype(F32) * gain[:, cols(i)]
        grad = (inverse * scaled - factor * raw[:, cols(i)]).astype(BF16)
        og[:, cols(i)] = grad
        query_decayed = (entries[i] * q[:, cols(i)].astype(F32)).astype(BF16)
        send_shares(1, i, dot(query_decayed, grad, 0, 0))

    results = []

    def deliver(source, target):
        j = len(results) // 2
        keep = pltpu.make_async_copy(source.at[own], target.at[:, mine], own_sem.at[j])
        send = remote(
            source.at[other_rows], target.at[:, mine], result_send.at[j], result_recv.at[j], sib
        )
        send.start()
        keep.start()
        results.extend((keep, send))

    for i in range(HALF):
        att[:, cols(i)] = (raw[:, cols(i)] * inverse * gain[:, cols(i)]).astype(BF16)
    deliver(att, att_out)
    for i in range(HALF):
        grad = og[:, cols(i)]
        dscore = (dot(grad, v[:, cols(i)], 1, 1) * table[i]).astype(BF16)
        dq[:, cols(i)] = (
            dot(dscore, k[:, cols(i)], 1, 0) + dot(grad, state(0, i), 1, 1) * entries[i]
        ).astype(BF16)
        dk_part[:, cols(i)] = dot(dscore, q[:, cols(i)], 0, 0)
        dv_part[:, cols(i)] = dot(weights[i], grad, 0, 0)
    deliver(dq, dq_out)

    turn(1, True)

    def finish(j, i, value, target):
        value = value.astype(BF16)
        place_at = pl.ds(pl.multiple_of(core * WIDE + i * HD, HD), HD)
        target[:, place_at] = jnp.where(is0, value[:TOK], value[TOK:])
        last[j, i] = jnp.where(is0, value[TOK:], value[:TOK])
        return remote(
            last.at[j, i], target.at[:, place_at], last_send.at[j, i], last_recv.at[j, i], sib
        )

    finals = []
    for i in use_order:
        arrived(1, i)
        add_early(i)
        grad_state = state(1, i)
        for j, (part, operand, side, target) in enumerate(
            ((dk_part, v, 1, dk_out), (dv_part, k, 0, dv_out))
        ):
            copy = finish(
                j,
                i,
                part[:, cols(i)] + dot(operand[:, cols(i)], grad_state, 1, side) * tails[i],
                target,
            )
            copy.start()
            finals.append(copy)

    for swap in swaps + [state_swap]:
        swap.wait_send()
    for copy in sum_copies:
        copy.wait_send()
    for phase in range(2):
        for other in ring:
            back_copy(phase, other).wait_send()
    for copy in results + finals:
        copy.wait()


def place_results(*refs):
    sources, targets, sems = refs[:4], refs[4:8], refs[8]
    copies = [
        pltpu.make_async_copy(src, dst, sems.at[i])
        for i, (src, dst) in enumerate(zip(sources, targets))
    ]
    for copy in copies:
        copy.start()
    for copy in copies:
        copy.wait()


def body(query_rows, key_rows, value_rows, out_grad, slopes, norm_gain, doc_lengths):
    rows, width = query_rows.shape
    features = width * lax.axis_size("tp")
    whole = jax.ShapeDtypeStruct((rows, width), BF16)
    in_hbm = pl.BlockSpec(memory_space=pltpu.HBM)
    in_vmem = pl.BlockSpec(memory_space=pltpu.VMEM)
    dma = pltpu.SemaphoreType.DMA
    pair_bf16 = pltpu.VMEM((PAIR, WIDE), BF16)
    pair_f32 = pltpu.VMEM((PAIR, WIDE), F32)
    shares = pltpu.VMEM((2, ZN, SHARE, HD), BF16)
    carry = pltpu.VMEM((2, SHARE, HD), BF16)
    results = pl.pallas_call(
        functools.partial(kernel, features),
        out_shape=(pltpu.VMEM((rows, width), BF16),) * 4,
        in_specs=[in_hbm] * 7,
        out_specs=(in_vmem,) * 4,
        scratch_shapes=[
            pltpu.SMEM(slopes.shape, F32),
            pltpu.SMEM(doc_lengths.shape, jnp.int32),
            pltpu.VMEM((width,), F32),
            pltpu.VMEM((1, WIDE), F32),
            pair_bf16,
            pair_bf16,
            pair_bf16,
            pair_bf16,
            pltpu.VMEM((TOK, WIDE), BF16),
            pltpu.VMEM((TOK, WIDE), BF16),
            pair_bf16,
            pair_bf16,
            pltpu.VMEM((2, HALF, TOK, HD), BF16),
            pltpu.VMEM((HALF, PAIR, HD), F32),
            pltpu.VMEM((HALF, PAIR, HD), F32),
            pltpu.VMEM((HALF, HD, HD), F32),
            pltpu.VMEM((HALF, HD, HD), BF16),
            pltpu.VMEM((HALF, HD, HD), BF16),
            pltpu.VMEM((HALF, PAIR, PAIR), F32),
            pltpu.VMEM((HALF, PAIR, PAIR), BF16),
            pair_f32,
            pair_f32,
            pair_f32,
            shares,
            shares,
            carry,
            carry,
            shares,
            shares,
            pltpu.VMEM((ZN, SHARE, HD), F32),
            pltpu.VMEM((4, ZN, 1, HD), F32),
            pltpu.VMEM((ZN, SHARE, HD), BF16),
            pltpu.VMEM((2 * XN, 8, HD), F32),
            pltpu.SemaphoreType.REGULAR((ZN + 2,)),
            dma((1,)),
            dma((ZN,)),
            dma((9,)),
            dma((2,)),
            dma((5,)),
            dma((5,)),
            dma((2, ZN)),
            dma((2, ZN)),
            dma((2,)),
            dma((2,)),
            dma((2, ZN)),
            dma((2, ZN)),
            dma((2 * XN,)),
            dma((2 * XN,)),
            dma((2,)),
            dma((2,)),
            dma((2, HALF)),
            dma((2, HALF)),
        ],
        compiler_params=pltpu.CompilerParams(
            collective_id=0, has_side_effects=True, vmem_limit_bytes=48 * 1024 * 1024
        ),
        name="lightning",
    )(
        *(
            pltpu.with_memory_space_constraint(a, pltpu.HBM)
            for a in (slopes, doc_lengths, query_rows, key_rows, value_rows, out_grad, norm_gain)
        )
    )
    return pl.pallas_call(
        place_results,
        out_shape=(whole,) * 4,
        in_specs=[in_vmem] * 4,
        out_specs=(in_hbm,) * 4,
        scratch_shapes=[dma((4,))],
        compiler_params=pltpu.CompilerParams(vmem_limit_bytes=8 * 1024 * 1024),
        name="place",
    )(*(pltpu.with_memory_space_constraint(a, pltpu.VMEM) for a in results))


def solution(mesh):
    spec = P("ctx", "tp")
    in_specs = (spec, spec, spec, spec, P("tp"), P("tp"), P())
    return jax.shard_map(
        body, mesh=mesh, in_specs=in_specs, out_specs=(spec,) * 4, check_vma=False
    )
```

```python
import functools

import jax
import jax.numpy as jnp
from jax import lax
from jax.experimental import pallas as pl
from jax.experimental.pallas import tpu as pltpu
from jax.sharding import PartitionSpec as P

HD = 128
EPSILON = 1e-06
MESH = pl.DeviceIdType.MESH
F32 = jnp.float32
BF16 = jnp.bfloat16
TOK = 128
PAIR = 2 * TOK
HALF = 4
WIDE = HALF * HD
ZN = 8
SHARE = HALF * HD // ZN
PER = ZN // HALF
XN = 4


def dot(a, b, ca, cb):
    return lax.dot_general(a, b, (((ca,), (cb,)), ((), ())), preferred_element_type=F32)


def kernel(
    features,
    slopes_hbm,
    doc_hbm,
    q_hbm,
    k_hbm,
    v_hbm,
    og_hbm,
    gain_hbm,
    att_out,
    dq_out,
    dk_out,
    dv_out,
    slopes,
    doc_lengths,
    gain_flat,
    gain,
    q,
    k,
    v,
    og,
    k_other,
    v_other,
    att,
    dq,
    last,
    entries,
    tails,
    local,
    local_other,
    local_in,
    table,
    weights,
    raw,
    dk_part,
    dv_part,
    share_out,
    share_in,
    carry_out,
    carry_in,
    back_out,
    back_in,
    kept,
    to_end_decay,
    early_in,
    sums,
    answers,
    early_send,
    early_recv,
    local_sem,
    own_sem,
    swap_send,
    swap_recv,
    share_send,
    share_recv,
    carry_send,
    carry_recv,
    back_send,
    back_recv,
    sums_send,
    sums_recv,
    result_send,
    result_recv,
    last_send,
    last_recv,
):
    ctx = lax.axis_index("ctx")
    x = lax.axis_index("tp")
    rows_y = lax.axis_size("ctx") // (2 * ZN)
    core = lax.rem(ctx, 2)
    z = lax.rem(ctx // 2, ZN)
    y = ctx // (2 * ZN)

    def device(dx, y_at, z_at, core_at):
        return (y_at * (2 * ZN) + z_at * 2 + core_at, lax.rem(x + dx, XN))

    sib = device(0, y, z, 1 - core)
    ring = [lax.rem(z + d, ZN) for d in (4, 3, 5, 2, 6, 1, 7)]
    heads_of = [(2, 1), (2, 0), (1, 1), (3, 1), (1, 0), (3, 0), (0, 1)]
    cross = [
        (2 * lax.rem(x + dx, XN) + lax.rem(core + dc, 2), device(dx, y, z, lax.rem(core + dc, 2)))
        for dx, dc in heads_of
    ]

    next_y, last_y = lax.rem(y + 1, rows_y), lax.rem(y + rows_y - 1, rows_y)

    def at_z(other):
        return device(0, y, other, core)

    def above(other):
        return device(0, next_y, other, core)

    def below(other):
        return device(0, last_y, other, core)


    mine = pl.ds(pl.multiple_of(core * WIDE, WIDE), WIDE)
    theirs = pl.ds(pl.multiple_of((1 - core) * WIDE, WIDE), WIDE)
    own = pl.ds(pl.multiple_of(core * TOK, TOK), TOK)
    other_rows = pl.ds(pl.multiple_of((1 - core) * TOK, TOK), TOK)

    loads = [
        pltpu.make_async_copy(src, dst, local_sem.at[i])
        for i, (src, dst) in enumerate(
            (
                (k_hbm.at[:, theirs], k_other),
                (v_hbm.at[:, theirs], v_other),
                (slopes_hbm, slopes),
                (doc_hbm, doc_lengths),
                (k_hbm.at[:, mine], k.at[own]),
                (v_hbm.at[:, mine], v.at[own]),
                (gain_hbm, gain_flat),
                (q_hbm.at[:, mine], q.at[own]),
                (og_hbm.at[:, mine], og.at[own]),
            )
        )
    ]
    for load in loads[:4]:
        load.start()

    barrier = pltpu.get_barrier_semaphore()
    along_z = [(other, at_z(other)) for other in ring]
    along_y = [(next_y, above(z)), (last_y, below(z))]
    along_x = [(index // 2, target) for index, target in cross[:-1]]

    def signal_if(condition, semaphore, target):
        @pl.when(condition)
        def _():
            pl.semaphore_signal(semaphore, 1, device_id=target, device_id_type=MESH)

    pl.semaphore_signal(barrier, 1, device_id=sib, device_id_type=MESH)
    for here, partners in ((z, along_z), (y, along_y), (x, along_x)):
        for other, target in partners:
            signal_if(other > here, barrier, target)
    for other, _ in along_z:
        signal_if((z == 0) & (other > 0), barrier, above(other))
    lower_y = (next_y < y).astype(jnp.int32) + (last_y < y).astype(jnp.int32)
    greetings = 1 + z + lower_y + 2 * x + (z > 0).astype(jnp.int32)

    def wait_some(semaphore, count):
        @pl.when(count > 0)
        def _():
            pl.semaphore_wait(semaphore, count)

    def answer():
        for other, target in along_z:
            signal_if(other < z, answers.at[z], target)
        for axis, here, partners in ((ZN, y, along_y), (ZN + 1, x, along_x)):
            for other, target in partners:
                signal_if(other < here, answers.at[axis], target)

    for load in loads[4:]:
        load.start()
    pl.semaphore_wait(barrier, greetings)
    answer()

    def remote(src, dst, send, recv, target):
        return pltpu.make_async_remote_copy(
            src_ref=src,
            dst_ref=dst,
            send_sem=send,
            recv_sem=recv,
            device_id=target,
            device_id_type=MESH,
        )

    swaps = [
        remote(src, dst.at[own], swap_send.at[i], swap_recv.at[i], sib)
        for i, (src, dst) in enumerate(
            ((k_other, k), (v_other, v), (q_hbm.at[:, theirs], q), (og_hbm.at[:, theirs], og))
        )
    ]
    state_swap = remote(local_other, local_in, swap_send.at[4], swap_recv.at[4], sib)

    for load in loads[2:4]:
        load.wait()

    starts = [jnp.int32(0)]
    for j in range(doc_lengths.shape[0] - 1):
        starts.append(starts[-1] + doc_lengths[j])

    def carries(block):
        hit = starts[0] == block
        for start in starts[1:]:
            hit = hit | (start == block)
        return jnp.where(hit, F32(0.0), F32(1.0))

    flag0 = carries(y * (2 * ZN) + 2 * z)
    flag1 = carries(y * (2 * ZN) + 2 * z + 1)
    slope = [slopes[HALF * core + i] for i in range(HALF)]
    def cols(i):
        return pl.ds(pl.multiple_of(i * HD, HD), HD)

    is0 = core == 0
    to_end = (TOK - 1.0) - lax.broadcasted_iota(jnp.int32, (TOK, HD), 0).astype(F32)
    to_end = to_end + jnp.where(is0, F32(TOK), F32(0.0))
    end_flag = jnp.where(is0, flag1, F32(1.0))

    def local_state(keys, values, head):
        kept = jnp.exp(-slopes[head] * to_end) * end_flag
        return dot(keys, (kept * values.astype(F32)).astype(BF16), 0, 0)

    loads[0].wait()
    loads[1].wait()
    for i in range(HALF):
        local_other[i] = local_state(
            k_other[:, cols(i)], v_other[:, cols(i)], HALF * (1 - core) + i
        ).astype(BF16)
    state_swap.start()
    loads[4].wait()
    loads[5].wait()
    for i in range(HALF):
        local[i] = local_state(k[own, cols(i)], v[own, cols(i)], HALF * core + i)

    far = lax.rem(z // PER + HALF // 2, HALF)
    near = z // PER
    between = [lax.rem(far + d, HALF) for d in (1, 3)]
    next_door = z + 1 - 2 * lax.rem(z, 2)
    send_order = [far] + between + [near]
    use_order = [near] + between[::-1] + [far]

    def shares_of(i):
        return [next_door] if i is near else [PER * i + j for j in range(PER)]

    def share_copy(phase, other):
        return remote(
            share_out.at[phase, other],
            share_in.at[phase, z],
            share_send.at[phase, other],
            share_recv.at[phase, z],
            at_z(other),
        )

    def share_arrival(phase, other):
        return remote(
            share_out.at[phase, z],
            share_in.at[phase, other],
            share_send.at[phase, other],
            share_recv.at[phase, other],
            at_z(other),
        )

    def back_copy(phase, other):
        return remote(
            back_out.at[phase, other],
            back_in.at[phase, z],
            back_send.at[phase, other],
            back_recv.at[phase, z],
            at_z(other),
        )

    def put_shares(phase, i, value):
        share_out[phase, pl.ds(PER * i, PER)] = value.astype(BF16).reshape(PER, SHARE, HD)

    def send_shares(phase, i, value):
        put_shares(phase, i, value)
        for other in shares_of(i):
            share_copy(phase, other).start()
        if i is near:
            share_in[phase, z] = share_out[phase, z]

    def early_copy():
        return remote(
            carry_out.at[1], early_in.at[z], early_send.at[0], early_recv.at[z], below(0)
        )

    def add_early(i):
        @pl.when(z == 0)
        def _():
            decay = jnp.exp(
                jnp.full((1, HD), -1.0 * PAIR * (ZN - 1), F32) * slopes[HALF * core + i]
            )
            decay = decay * row_flag
            for share in shares_of(i):
                remote(
                    carry_out.at[1],
                    early_in.at[share],
                    early_send.at[0],
                    early_recv.at[share],
                    sib,
                ).wait_recv()
                back_in[1, share] = (
                    back_in[1, share].astype(F32) + decay * early_in[share].astype(F32)
                ).astype(BF16)

    def turn(phase, backward):
        total = share_in[phase, z].astype(F32) * to_end_decay[phase, z]
        for other in ring[::-1]:
            share_arrival(phase, other).wait_recv()
            total = total + share_in[phase, other].astype(F32) * to_end_decay[phase, other]
        carry_out[phase] = total.astype(BF16)
        carry = remote(
            carry_out.at[phase],
            carry_in.at[phase],
            carry_send.at[phase],
            carry_recv.at[phase],
            below(z) if backward else above(z),
        )
        if backward:

            @pl.when(z != 0)
            def _():
                early_copy().start()

        carry.start()
        inside = jnp.zeros((SHARE, HD), F32)
        for j in range(ZN - 1, -1, -1) if backward else range(ZN):
            kept[j] = inside
            inside = inside * step_decay[j] + share_in[phase, j].astype(F32)
        if backward:
            back_out[1, 0] = kept[0].astype(BF16)

            @pl.when(z != 0)
            def _():
                back_copy(1, 0).start()

        carry.wait_recv()
        incoming = carry_in[phase].astype(F32)
        if backward:
            for other in range(1, ZN):
                back_out[phase, other] = (
                    kept[other] + to_end_decay[2 + phase, other] * incoming
                ).astype(BF16)

                @pl.when(other != z)
                def _():
                    back_copy(phase, other).start()

        else:
            for other in ring:
                back_out[phase, other] = (
                    kept[other] + to_end_decay[2 + phase, other] * incoming
                ).astype(BF16)
                back_copy(phase, other).start()
        back_in[phase, z] = (kept[z] + to_end_decay[2 + phase, z] * incoming).astype(BF16)
        for other in ring:
            share_copy(phase, other).wait_send()
        carry.wait_send()
        if backward:

            @pl.when(z != 0)
            def _():
                early_copy().wait_send()

    def arrived(phase, i):
        for other in shares_of(i):
            remote(
                back_out.at[phase, z],
                back_in.at[phase, other],
                back_send.at[phase, other],
                back_recv.at[phase, other],
                at_z(other),
            ).wait_recv()
        return state(phase, i)

    def state(phase, i):
        return back_in[phase, pl.ds(PER * i, PER)].reshape(HD, HD)

    state_swap.wait_recv()
    for i in range(HALF):
        put_shares(0, i, local[i] + local_in[i].astype(F32))
    share_in[0, z] = share_out[0, z]
    for other in ring:

        @pl.when(other < z)
        def _():
            share_copy(0, other).start()

    for other in range(1, ZN):

        @pl.when(other > z)
        def _():
            pl.semaphore_wait(answers.at[other], 1)
            share_copy(0, other).start()

    for swap in swaps:
        swap.start()

    share_slope = slopes[HALF * core + z // PER]
    lam2 = jnp.exp(jnp.full((1, HD), -1.0 * PAIR, F32) * share_slope)
    row_flags = [
        carries(y * (2 * ZN) + 2 * j) * carries(y * (2 * ZN) + 2 * j + 1) for j in range(ZN)
    ]
    step_decay = [lam2 * flag for flag in row_flags]
    row_flag = row_flags[1]
    for j in range(2, ZN):
        row_flag = row_flag * row_flags[j]

    after, ahead = jnp.ones((1, HD), F32), jnp.ones((1, HD), F32)
    for j in range(ZN):
        to_end_decay[1, j] = after
        to_end_decay[2, j] = after
        to_end_decay[0, ZN - 1 - j] = ahead
        to_end_decay[3, ZN - 1 - j] = ahead
        after = after * step_decay[j]
        ahead = ahead * step_decay[ZN - 1 - j]

    loads[6].wait()
    for i in range(HALF):
        begin = pl.multiple_of(core * WIDE + i * HD, HD)
        gain[:, i * HD : (i + 1) * HD] = gain_flat[pl.ds(begin, HD)].reshape(1, HD)
    token = lax.broadcasted_iota(jnp.int32, (PAIR, HD), 0)
    second = token >= TOK
    token_f = token.astype(F32)
    entry_flag = jnp.where(second, flag0 * flag1, flag0)
    tail_flag = jnp.where(second, 1.0, flag1)
    row = lax.broadcasted_iota(jnp.int32, (PAIR, PAIR), 0)
    column = lax.broadcasted_iota(jnp.int32, (PAIR, PAIR), 1)
    distance = (row - column).astype(F32)
    reach = jnp.where((row >= TOK) & (column < TOK), flag1, 1.0)
    for i in range(HALF):
        entries[i] = jnp.exp(-slope[i] * (token_f + 1.0)) * entry_flag
        tails[i] = jnp.exp(-slope[i] * (PAIR - 1.0 - token_f)) * tail_flag
        table[i] = jnp.where(
            distance >= 0.0, jnp.exp(-slope[i] * jnp.maximum(distance, 0.0)) * reach, 0.0
        )
    for load in loads[7:]:
        load.wait()
    for swap in swaps:
        swap.wait_recv()
    for i in range(HALF):
        weight = (dot(q[:, cols(i)], k[:, cols(i)], 1, 1) * table[i]).astype(BF16)
        weights[i] = weight
        raw[:, cols(i)] = dot(weight, v[:, cols(i)], 1, 0)

    wait_some(answers.at[ZN], 2 - lower_y)
    turn(0, False)
    squares = jnp.zeros((PAIR, HD), F32)
    products = jnp.zeros((PAIR, HD), F32)
    for i in use_order:
        raw_i = raw[:, cols(i)] + dot(q[:, cols(i)], arrived(0, i), 1, 0) * entries[i]
        raw[:, cols(i)] = raw_i
        squares = squares + raw_i * raw_i
        products = products + raw_i * (og[:, cols(i)].astype(F32) * gain[:, cols(i)])

    def token_row(values):
        return jnp.sum(values.T, axis=0, keepdims=True)

    place = lax.broadcasted_iota(jnp.int32, (8, HD), 0)
    slot = 2 * x + core
    sums[slot] = jnp.where(
        place < 4,
        jnp.where(place < 2, token_row(squares[:TOK]), token_row(squares[TOK:])),
        jnp.where(place < 6, token_row(products[:TOK]), token_row(products[TOK:])),
    )
    wait_some(answers.at[ZN + 1], 2 * (XN - 1 - x))
    sum_copies = []
    for index, target in cross:
        copy = remote(
            sums.at[slot], sums.at[slot], sums_send.at[index], sums_recv.at[slot], target
        )
        copy.start()
        sum_copies.append(copy)
    for index, target in cross[::-1]:
        remote(
            sums.at[slot], sums.at[index], sums_send.at[index], sums_recv.at[index], target
        ).wait_recv()
    total = sums[0]
    for j in range(1, 2 * XN):
        total = total + sums[j]
    inverse_rows = lax.rsqrt(total[0:4] / features + EPSILON)
    factor_rows = inverse_rows * inverse_rows * inverse_rows * total[4:8] / features

    def token_columns(rows):
        return jnp.concatenate(
            [jnp.broadcast_to(rows[j : j + 1], (HD, HD)).T for j in (0, 2)], axis=0
        )

    inverse = token_columns(inverse_rows)
    factor = token_columns(factor_rows)

    for i in send_order:
        scaled = og[:, cols(i)].astype(F32) * gain[:, cols(i)]
        grad = (inverse * scaled - factor * raw[:, cols(i)]).astype(BF16)
        og[:, cols(i)] = grad
        query_decayed = (entries[i] * q[:, cols(i)].astype(F32)).astype(BF16)
        send_shares(1, i, dot(query_decayed, grad, 0, 0))

    results = []

    def deliver(source, target):
        j = len(results) // 2
        keep = pltpu.make_async_copy(source.at[own], target.at[:, mine], own_sem.at[j])
        send = remote(
            source.at[other_rows], target.at[:, mine], result_send.at[j], result_recv.at[j], sib
        )
        send.start()
        keep.start()
        results.extend((keep, send))

    for i in range(HALF):
        att[:, cols(i)] = (raw[:, cols(i)] * inverse * gain[:, cols(i)]).astype(BF16)
    deliver(att, att_out)
    for i in range(HALF):
        grad = og[:, cols(i)]
        dscore = (dot(grad, v[:, cols(i)], 1, 1) * table[i]).astype(BF16)
        dq[:, cols(i)] = (
            dot(dscore, k[:, cols(i)], 1, 0) + dot(grad, state(0, i), 1, 1) * entries[i]
        ).astype(BF16)
        dk_part[:, cols(i)] = dot(dscore, q[:, cols(i)], 0, 0)
        dv_part[:, cols(i)] = dot(weights[i], grad, 0, 0)
    deliver(dq, dq_out)

    turn(1, True)

    def finish(j, i, value, target):
        value = value.astype(BF16)
        place_at = pl.ds(pl.multiple_of(core * WIDE + i * HD, HD), HD)
        target[:, place_at] = jnp.where(is0, value[:TOK], value[TOK:])
        last[j, i] = jnp.where(is0, value[TOK:], value[:TOK])
        return remote(
            last.at[j, i], target.at[:, place_at], last_send.at[j, i], last_recv.at[j, i], sib
        )

    finals = []
    for i in use_order:
        arrived(1, i)
        add_early(i)
        grad_state = state(1, i)
        for j, (part, operand, side, target) in enumerate(
            ((dk_part, v, 1, dk_out), (dv_part, k, 0, dv_out))
        ):
            copy = finish(
                j,
                i,
                part[:, cols(i)] + dot(operand[:, cols(i)], grad_state, 1, side) * tails[i],
                target,
            )
            copy.start()
            finals.append(copy)

    for swap in swaps + [state_swap]:
        swap.wait_send()
    for copy in sum_copies:
        copy.wait_send()
    for phase in range(2):
        for other in ring:
            back_copy(phase, other).wait_send()
    for copy in results + finals:
        copy.wait()


def place_results(*refs):
    sources, targets, sems = refs[:4], refs[4:8], refs[8]
    copies = [
        pltpu.make_async_copy(src, dst, sems.at[i])
        for i, (src, dst) in enumerate(zip(sources, targets))
    ]
    for copy in copies:
        copy.start()
    for copy in copies:
        copy.wait()


def body(query_rows, key_rows, value_rows, out_grad, slopes, norm_gain, doc_lengths):
    rows, width = query_rows.shape
    features = width * lax.axis_size("tp")
    whole = jax.ShapeDtypeStruct((rows, width), BF16)
    in_hbm = pl.BlockSpec(memory_space=pltpu.HBM)
    in_vmem = pl.BlockSpec(memory_space=pltpu.VMEM)
    dma = pltpu.SemaphoreType.DMA
    pair_bf16 = pltpu.VMEM((PAIR, WIDE), BF16)
    pair_f32 = pltpu.VMEM((PAIR, WIDE), F32)
    shares = pltpu.VMEM((2, ZN, SHARE, HD), BF16)
    carry = pltpu.VMEM((2, SHARE, HD), BF16)
    results = pl.pallas_call(
        functools.partial(kernel, features),
        out_shape=(pltpu.VMEM((rows, width), BF16),) * 4,
        in_specs=[in_hbm] * 7,
        out_specs=(in_vmem,) * 4,
        scratch_shapes=[
            pltpu.SMEM(slopes.shape, F32),
            pltpu.SMEM(doc_lengths.shape, jnp.int32),
            pltpu.VMEM((width,), F32),
            pltpu.VMEM((1, WIDE), F32),
            pair_bf16,
            pair_bf16,
            pair_bf16,
            pair_bf16,
            pltpu.VMEM((TOK, WIDE), BF16),
            pltpu.VMEM((TOK, WIDE), BF16),
            pair_bf16,
            pair_bf16,
            pltpu.VMEM((2, HALF, TOK, HD), BF16),
            pltpu.VMEM((HALF, PAIR, HD), F32),
            pltpu.VMEM((HALF, PAIR, HD), F32),
            pltpu.VMEM((HALF, HD, HD), F32),
            pltpu.VMEM((HALF, HD, HD), BF16),
            pltpu.VMEM((HALF, HD, HD), BF16),
            pltpu.VMEM((HALF, PAIR, PAIR), F32),
            pltpu.VMEM((HALF, PAIR, PAIR), BF16),
            pair_f32,
            pair_f32,
            pair_f32,
            shares,
            shares,
            carry,
            carry,
            shares,
            shares,
            pltpu.VMEM((ZN, SHARE, HD), F32),
            pltpu.VMEM((4, ZN, 1, HD), F32),
            pltpu.VMEM((ZN, SHARE, HD), BF16),
            pltpu.VMEM((2 * XN, 8, HD), F32),
            pltpu.SemaphoreType.REGULAR((ZN + 2,)),
            dma((1,)),
            dma((ZN,)),
            dma((9,)),
            dma((2,)),
            dma((5,)),
            dma((5,)),
            dma((2, ZN)),
            dma((2, ZN)),
            dma((2,)),
            dma((2,)),
            dma((2, ZN)),
            dma((2, ZN)),
            dma((2 * XN,)),
            dma((2 * XN,)),
            dma((2,)),
            dma((2,)),
            dma((2, HALF)),
            dma((2, HALF)),
        ],
        compiler_params=pltpu.CompilerParams(
            collective_id=0, has_side_effects=True, vmem_limit_bytes=48 * 1024 * 1024
        ),
        name="lightning",
    )(
        *(
            pltpu.with_memory_space_constraint(a, pltpu.HBM)
            for a in (slopes, doc_lengths, query_rows, key_rows, value_rows, out_grad, norm_gain)
        )
    )
    return pl.pallas_call(
        place_results,
        out_shape=(whole,) * 4,
        in_specs=[in_vmem] * 4,
        out_specs=(in_hbm,) * 4,
        scratch_shapes=[dma((4,))],
        compiler_params=pltpu.CompilerParams(vmem_limit_bytes=8 * 1024 * 1024),
        name="place",
    )(*(pltpu.with_memory_space_constraint(a, pltpu.VMEM) for a in results))


def solution(mesh):
    spec = P("ctx", "tp")
    in_specs = (spec, spec, spec, spec, P("tp"), P("tp"), P())
    return jax.shard_map(
        body, mesh=mesh, in_specs=in_specs, out_specs=(spec,) * 4, check_vma=False
    )
```
